256 devices in a mesh: dp: 32 (over x, y, core), tensor: 8 (over z).
Axes of the slice: x: 4, y: 4, z: 8, core: 2. Of those that a mesh axis runs over, the one named last changes fastest.
Arguments:
- tokens: bfloat16 [65536, 5120], P('dp', 'tensor'), may hold values from -6 to 6
- cotangent: bfloat16 [65536, 1024], P('dp', 'tensor'), may hold values from -6 to 6
- base_weight: bfloat16 [5120, 1024], P('tensor'), may hold values from -0.078125 to 0.078125
- adapter_down: float32 [128, 5120, 64], P('dp', 'tensor'), may hold values from -0.078125 to 0.078125
- adapter_up: float32 [128, 64, 1024], P('dp', None, 'tensor'), may hold values from -0.75 to 0.75
- block_adapter: int32 [512], P('dp'), may hold values from 0 to 127, as said below
- adapter_slot: int32 [128], replicated, may hold values from 0 to 127, as said below
- adapter_rank: int32 [128], replicated, may hold values from 16 to 64, as said below
Outputs:
- values: bfloat16 [65536, 1024], P('dp', 'tensor')
- token_input_gradient: bfloat16 [65536, 5120], P('dp', 'tensor')
- down_matrix_gradient: float32 [128, 5120, 64], P('dp', 'tensor')
- up_matrix_gradient: float32 [128, 64, 1024], P('dp', None, 'tensor')
The draws below stay inside these ranges and needn't reach their ends.
Inputs may be any that keep to these rules, and one draw needn't show every extreme that they name: adapter_slot is a permutation; the owner of slot s is index s // 4 of dp. `block_adapter`: among the 16 blocks of one index of dp, at most 1 name adapters of any one owner; in every draw one owner gets exactly 1 block from every index of dp. `adapter_rank`: each rank is a multiple of 16.
All inputs are finite; a program needn't handle non-finite values.
Results may differ from the reference program's by a relative error of at most 0.02.
Values may be sent and summed in bfloat16 or wider, within the bound.
A program may use at most 128 MiB of HBM per device.

```python
import jax
import jax.numpy as jnp
from jax import lax

MODEL_WIDTH = 5120
VALUE_OUTPUTS = 1024
R = 64
BLOCK = 128
BLK_DEV = 16
ADP_DEV = 4
TOKEN_TOTAL = 65536
BLOCK_TOTAL = 512
ADAPTERS = 128
CAP = 1
N_TENSOR = 8


def shared_layout(key):
    slot_order = jax.random.permutation(jax.random.fold_in(key, 101), ADAPTERS).astype(jnp.int32)
    holder = jnp.argsort(slot_order).astype(jnp.int32)
    sources = BLOCK_TOTAL // BLK_DEV
    hottest = jax.random.randint(jax.random.fold_in(key, 102), (), 0, sources)
    source_keys = jax.random.split(jax.random.fold_in(key, 103), sources)

    def owner_order(one_key):
        scores = jax.random.permutation(one_key, sources).astype(jnp.int32) + 1
        scores = jnp.where(jnp.arange(sources) == hottest, 0, scores)
        return jnp.argsort(scores).astype(jnp.int32)
    orders = jax.vmap(owner_order)(source_keys)
    owner_of = orders[:, jnp.arange(BLK_DEV) // CAP]
    local_index = jax.random.randint(jax.random.fold_in(key, 104), (sources, BLK_DEV), 0, ADP_DEV)
    adapter_ids = holder[owner_of * ADP_DEV + local_index]
    shuffle_keys = jax.random.split(jax.random.fold_in(key, 105), sources)

    def shuffle_one(one_key):
        return jax.random.permutation(one_key, BLK_DEV).astype(jnp.int32)
    shuffles = jax.vmap(shuffle_one)(shuffle_keys)
    adapter_ids = jnp.take_along_axis(adapter_ids, shuffles, axis=1)
    return (slot_order, adapter_ids.reshape(BLOCK_TOTAL).astype(jnp.int32))


def draw_adapter_slot(key, part):
    return shared_layout(key)[0]


def draw_block_adapter(key, part):
    return shared_layout(key)[1]


def draw_adapter_rank(key, part):
    key = jax.random.fold_in(key, 7)
    rank_units = jax.random.randint(key, (ADAPTERS,), 1, 5)
    rank_units = rank_units.at[0].set(4).at[1].set(1)
    return (rank_units * (R // 4)).astype(jnp.int32)


def level_of(key, shape, pieces, least, high):
    loudness, own = 1.0, jax.random.fold_in(key, 6)
    for dim, blocks in pieces:
        heights = jnp.exp(jax.random.uniform(jax.random.fold_in(own, dim), (blocks,), jnp.float32, least / len(pieces), high / len(pieces)))
        loudness = loudness * jnp.repeat(heights, shape[dim] // blocks).reshape([-1 if axis == dim else 1 for axis in range(len(shape))])
    return loudness


def noise(own_key, extent, spread, most, pieces=(), kind=jnp.bfloat16):
    array = spread * jax.random.normal(own_key, extent, jnp.float32)
    if pieces:
        array = array * level_of(own_key, extent, pieces, -0.22, 0.18)
    return jnp.clip(array, -most, most).astype(kind)


def setup_inputs(seed: int = 0) -> dict:
    seeds = jax.random.split(jax.random.key(seed), 9)
    return {
        "tokens": noise(seeds[0], (TOKEN_TOTAL, MODEL_WIDTH), 1.0, 6.0, ((0, 32), (1, 8))),
        "cotangent": noise(seeds[1], (TOKEN_TOTAL, VALUE_OUTPUTS), 1.0, 6.0, ((0, 32), (1, 8))),
        "base_weight": noise(seeds[2], (MODEL_WIDTH, VALUE_OUTPUTS), MODEL_WIDTH ** -0.5, 0.078125, ((0, 8),)),
        "adapter_down": noise(seeds[3], (ADAPTERS, MODEL_WIDTH, R), MODEL_WIDTH ** -0.5, 0.078125, ((0, 32), (1, 8)), jnp.float32),
        "adapter_up": noise(seeds[4], (ADAPTERS, R, VALUE_OUTPUTS), R ** -0.5, 0.75, ((0, 32), (2, 8)), jnp.float32),
        "block_adapter": draw_block_adapter(jax.random.fold_in(seeds[8], 71), 0),
        "adapter_slot": draw_adapter_slot(jax.random.fold_in(seeds[8], 71), 0),
        "adapter_rank": draw_adapter_rank(jax.random.fold_in(seeds[8], 71), 0),
    }


def reference(tokens, cotangent, base_weight, adapter_down, adapter_up, block_adapter, adapter_slot, adapter_rank):
    group_width = MODEL_WIDTH // N_TENSOR
    frozen_value_rows = jnp.zeros((TOKEN_TOTAL, VALUE_OUTPUTS), jnp.float32)
    for shard_index in range(N_TENSOR):
        lower = shard_index * group_width
        partial_term = jnp.dot(tokens[:, lower:lower + group_width], base_weight[lower:lower + group_width], preferred_element_type=jnp.float32)
        rounded = lax.optimization_barrier(partial_term.astype(jnp.bfloat16))
        frozen_value_rows = frozen_value_rows + rounded.astype(jnp.float32)
    frozen_gradient_rows = lax.dot_general(cotangent, base_weight, (((1,), (1,)), ((), ())), preferred_element_type=jnp.float32)

    def per_block_update(running, block_index):
        down_gradient_total, up_gradient_total = running
        adapter = block_adapter[block_index]
        slot_here = adapter_slot[adapter].astype(jnp.int32)
        rank_here = adapter_rank[adapter]
        active = (jnp.arange(R) < rank_here).astype(jnp.float32)
        scaling = R / (4.0 * rank_here.astype(jnp.float32))
        down_matrix_narrow = (adapter_down[slot_here] * active[None, :]).astype(jnp.bfloat16)
        up_matrix_narrow = (adapter_up[slot_here] * active[:, None]).astype(jnp.bfloat16)
        start_row = (block_index * BLOCK).astype(jnp.int32)
        block_tokens = lax.dynamic_slice_in_dim(tokens, start_row, BLOCK, 0)
        block_cot = lax.dynamic_slice_in_dim(cotangent, start_row, BLOCK, 0)
        low_full = jnp.dot(block_tokens, down_matrix_narrow, preferred_element_type=jnp.float32)
        reduced_scaled_rows = (scaling * low_full).astype(jnp.bfloat16)
        back_full = lax.dot_general(block_cot, up_matrix_narrow, (((1,), (1,)), ((), ())), preferred_element_type=jnp.float32)
        backward_scaled_rows = (scaling * back_full).astype(jnp.bfloat16)
        adapter_value_rows = jnp.dot(reduced_scaled_rows, up_matrix_narrow, preferred_element_type=jnp.float32).astype(jnp.bfloat16)
        adapter_gradient_rows = lax.dot_general(backward_scaled_rows, down_matrix_narrow, (((1,), (1,)), ((), ())), preferred_element_type=jnp.float32).astype(jnp.bfloat16)
        down_piece = lax.dot_general(block_tokens, backward_scaled_rows, (((0,), (0,)), ((), ())), preferred_element_type=jnp.float32)
        up_piece = lax.dot_general(reduced_scaled_rows, block_cot, (((0,), (0,)), ((), ())), preferred_element_type=jnp.float32)
        down_gradient_total = down_gradient_total.at[slot_here].add(down_piece)
        up_gradient_total = up_gradient_total.at[slot_here].add(up_piece)
        return (down_gradient_total, up_gradient_total), (adapter_value_rows, adapter_gradient_rows)

    initial_carry_state = (jnp.zeros((ADAPTERS, MODEL_WIDTH, R), jnp.float32), jnp.zeros((ADAPTERS, R, VALUE_OUTPUTS), jnp.float32))
    (down_matrix_gradient, up_matrix_gradient), (adapter_value_rows, adapter_gradient_rows) = lax.scan(per_block_update, initial_carry_state, jnp.arange(BLOCK_TOTAL, dtype=jnp.int32))
    adapter_value_rows = lax.optimization_barrier(adapter_value_rows.reshape(TOKEN_TOTAL, VALUE_OUTPUTS))
    adapter_gradient_rows = lax.optimization_barrier(adapter_gradient_rows.reshape(TOKEN_TOTAL, MODEL_WIDTH))
    values = (frozen_value_rows + adapter_value_rows.astype(jnp.float32)).astype(jnp.bfloat16)
    token_input_gradient = (frozen_gradient_rows + adapter_gradient_rows.astype(jnp.float32)).astype(jnp.bfloat16)
    return values, token_input_gradient, down_matrix_gradient, up_matrix_gradient
```

```python
import functools

import jax
import jax.numpy as jnp
from jax import lax
from jax.experimental import pallas as pl
from jax.experimental.pallas import tpu as pltpu
from jax.sharding import PartitionSpec as P

MESH = pl.DeviceIdType.MESH
BF, F32, I32 = jnp.bfloat16, jnp.float32, jnp.int32
DP, NZ = 32, 8
ROWS, FEAT, HEAD, R, BLK, NB, OWN = 2048, 640, 128, 64, 128, 16, 4
CH = 256
NC = ROWS // CH
MSG = 3 * NC + NC // 2
DEPTH = 4
LAST = MSG // 2
T_UP = 4
T_BACK = T_UP + 1
T_DOWN = 16
T_LOW = T_DOWN + 1


def dot(a, b, ca, cb):
    return lax.dot_general(a, b, (((ca,), (cb,)), ((), ())), preferred_element_type=F32)


def kernel(
    ba_s, slot_s, rank_s, slot_v, rank_v, tok_h, cot_h, w_h, dn_h, up_h,
    val_o, tig_o, dmg_o, umg_o,
    tok, cotf, w, dnf, upf, dnb, upb, base, rsr, reqs, tagr, tag_v, bi_v, scale,
    usend, urecv, dsend, drecv, gsend, grecv, hsend, hrecv, grads, hgrads,
    arp, arr, tot, scaled, lorav, valv, tigv, dacc, uacc, tag_s, bi_s,
    in_sem, out_sem, ag_s, ag_r, rs_s, rs_r, ar_s, ar_r, tg_s, tg_r,
    us_s, us_r, ds_s, ds_r, gs_s, gs_r, hs_s, hs_r, sm_sem,
):
    d = lax.axis_index("dp")
    z = lax.axis_index("tensor")
    x, y, c = d // 8, (d // 2) % 4, d % 2
    right, left = (z + 1) % NZ, (z + NZ - 1) % NZ

    cp_cot = pltpu.make_async_copy(cot_h, cotf.at[z], in_sem.at[0])
    cp_up = pltpu.make_async_copy(up_h, upf, in_sem.at[1])
    cp_dn = pltpu.make_async_copy(dn_h, dnf, in_sem.at[2])
    cp_tok = pltpu.make_async_copy(tok_h, tok, in_sem.at[3])
    cp_w = pltpu.make_async_copy(w_h, w, in_sem.at[4])
    for cp in (cp_cot, cp_up, cp_dn, cp_tok, cp_w):
        cp.start()

    barrier = pltpu.get_barrier_semaphore()

    def greet(i, carry):
        pl.semaphore_signal(barrier, inc=1, device_id=((d + i) % DP, z), device_id_type=MESH)
        return carry

    lax.fori_loop(1, DP, greet, 0)
    for to in (right, left):
        pl.semaphore_signal(barrier, inc=1, device_id=(d, to), device_id_type=MESH)

    own3 = lax.broadcasted_iota(I32, (DP, 8, 128), 0)
    own2 = lax.broadcasted_iota(I32, (DP, 128), 0)
    pair2 = lax.broadcasted_iota(I32, (8, 128), 0)
    lane2 = lax.broadcasted_iota(I32, (8, 128), 1)
    tags = jnp.zeros((DP, 8, 128), I32)
    which = jnp.zeros((DP, 128), I32)
    ranks = jnp.ones((8, 128), I32)
    for b in range(NB):
        a = ba_s[b]
        s = slot_s[a]
        o = s // OWN
        tags = jnp.where(own3 == o, s - o * OWN + 1, tags)
        which = jnp.where(own2 == o, b, which)
        here = (pair2 == b // 2) & ((lane2 >= R) if b % 2 else (lane2 < R))
        ranks = jnp.where(here, rank_s[a], ranks)
    reqs[...] = tags
    bi_v[...] = which
    scale[...] = R / (4.0 * ranks.astype(F32))
    cp_bi = pltpu.make_async_copy(bi_v, bi_s, sm_sem.at[0])
    cp_bi.start()
    pl.semaphore_wait(barrier, DP + 1)

    def ag(m, dirn):
        h, cc = m // NC, m % NC
        row = cc * CH
        if dirn == 0:
            shard, to = (z - h + NZ) % NZ, right
        else:
            shard, to = (z + h) % NZ, left
            row = row + (h // 3) * (ROWS // 2)
        part = cotf.at[shard, pl.ds(pl.multiple_of(row, CH), CH)]
        return pltpu.make_async_remote_copy(
            src_ref=part, dst_ref=part, send_sem=ag_s.at[dirn, m], recv_sem=ag_r.at[dirn, m],
            device_id=(d, to), device_id_type=MESH)

    cp_cot.wait()

    def ag_first(m, carry):
        ag(m, 0).start()
        ag(m, 1).start()
        return carry

    lax.fori_loop(0, DEPTH, ag_first, 0)

    def xmsg(i, src, dst, ss, rs):
        j = (i * 13) % DP
        px, py, pc = (x + j // 8) % 4, (y + (j // 2) % 4) % 4, (c + j % 2) % 2
        t = px * 8 + py * 2 + pc
        return t, pltpu.make_async_remote_copy(
            src_ref=src.at[t], dst_ref=dst.at[d], send_sem=ss.at[i], recv_sem=rs.at[i],
            device_id=(t, z), device_id_type=MESH)

    def x_recv(src, dst, ss, rs):
        def go(i, carry):
            xmsg(i, src, dst, ss, rs)[1].wait_recv()
            return carry
        lax.fori_loop(1, DP, go, 0)

    def x_sent(src, dst, ss, rs):
        def go(i, carry):
            xmsg(i, src, dst, ss, rs)[1].wait_send()
            return carry
        lax.fori_loop(1, DP, go, 0)

    tg = (reqs, tagr, tg_s, tg_r)
    us = (usend, urecv, us_s, us_r)
    ds = (dsend, drecv, ds_s, ds_r)
    gs = (gsend, grecv, gs_s, gs_r)
    hs = (hsend, hrecv, hs_s, hs_r)

    def tag_go(i, carry):
        xmsg(i, *tg)[1].start()
        return carry

    lax.fori_loop(1, DP, tag_go, 0)
    tagr[d] = reqs[d]

    cp_up.wait()
    cp_dn.wait()
    for l in range(OWN):
        mine = slot_v[...] == d * OWN + l
        rank = jnp.sum(jnp.where(mine, rank_v[...], 0), axis=1, keepdims=True)
        upb[l] = jnp.where(lax.broadcasted_iota(I32, (R, HEAD), 0) < rank, upf[l], 0.0).astype(BF)
        dnb[l] = jnp.where(lax.broadcasted_iota(I32, (R, FEAT), 0) < rank, dnf[l], 0.0).astype(BF)
    x_recv(*tg)
    tag_v[...] = tagr[:, 0, :]
    cp_tag = pltpu.make_async_copy(tag_v, tag_s, sm_sem.at[1])
    cp_tag.start()
    cp_tag.wait()

    def fill(src, args):
        def go(i, carry):
            t, copy = xmsg(i, *args)
            args[0][t] = src[jnp.maximum(tag_s[t, 0] - 1, 0)]
            copy.start()
            return carry
        lax.fori_loop(1, DP, go, 0)
        args[1][d] = src[jnp.maximum(tag_s[d, 0] - 1, 0)]

    fill(upb, us)
    fill(dnb, ds)
    cp_bi.wait()
    cp_tok.wait()
    cp_w.wait()

    def owner_of(b):
        return slot_s[ba_s[b]] // OWN

    half = (slice(0, BLK // 2), slice(BLK // 2, BLK))

    def ar_copy(q, k, dirn, src, dst):
        return pltpu.make_async_remote_copy(
            src_ref=src, dst_ref=dst, send_sem=ar_s.at[q, dirn, k], recv_sem=ar_r.at[q, dirn, k],
            device_id=(d, (right, left)[dirn]), device_id_type=MESH)

    def ar_msg(q, k, dirn):
        sgn = (1, -1)[dirn]
        if k == 0:
            p = (z + 4) % NZ
            lo = (0, BLK // 2)[dirn]
            return ar_copy(q, k, dirn, arp.at[q, p, pl.ds(lo, BLK // 2)], arr.at[q, dirn, 0, pl.ds(lo, BLK // 2)])
        if k < 4:
            p = (z + sgn * (4 - k) + NZ) % NZ
            return ar_copy(q, k, dirn, arp.at[q, p], arr.at[q, dirn, k])
        p = (z - sgn * (k - 4) + NZ) % NZ
        if k < 7:
            return ar_copy(q, k, dirn, tot.at[q, p], tot.at[q, p])
        lo = (0, BLK // 2)[dirn]
        part = tot.at[q, p, pl.ds(lo, BLK // 2)]
        return ar_copy(q, k, dirn, part, part)

    def ar_step(q, k):
        if k > 0:
            for dirn in (0, 1):
                ar_msg(q, k - 1, dirn).wait_recv()
        if k in (1, 2, 3):
            for dirn in (0, 1):
                p = (z + (1, -1)[dirn] * (4 - k) + NZ) % NZ
                rows = half[dirn] if k == 1 else slice(0, BLK)
                arp[q, p, rows] = (arp[q, p, rows].astype(F32) + arr[q, dirn, k - 1, rows].astype(F32)).astype(BF)
        if k == 4:
            tot[q, z] = (arp[q, z].astype(F32) + arr[q, 0, 3].astype(F32) + arr[q, 1, 3].astype(F32)).astype(BF)
        if k < 8:
            for dirn in (0, 1):
                ar_msg(q, k, dirn).start()

    def scale_all(q):
        def go(j, carry):
            scaled[q, j] = (scale[pl.ds(j, 1), :] * tot[q, j].astype(F32)).astype(BF)
            return carry
        lax.fori_loop(0, NZ, go, 0)

    lanes = lax.broadcasted_iota(I32, (BLK, 2 * R), 1)

    def rows_of(b, n=BLK):
        return pl.ds(pl.multiple_of(b * n, n), n)

    def back_partial():
        x_recv(*us)

        def go(j, carry):
            parts = []
            for k in (0, 1):
                b = 2 * j + k
                parts.append(dot(cotf[z, rows_of(b), :], urecv[owner_of(b)], 1, 1))
            arp[0, j] = jnp.concatenate(parts, axis=1).astype(BF)
            return carry

        lax.fori_loop(0, NZ, go, 0)

    def low_partial():
        x_recv(*ds)

        def go(j, carry):
            parts = []
            for k in (0, 1):
                b = 2 * j + k
                parts.append(dot(tok[rows_of(b), :], drecv[owner_of(b)], 1, 1))
            arp[1, j] = jnp.concatenate(parts, axis=1).astype(BF)
            return carry

        lax.fori_loop(0, NZ, go, 0)

    def send_grads(src, args):
        def go(i, carry):
            t, copy = xmsg(i, *args)
            args[0][t] = src[bi_s[t, 0]]
            copy.start()
            return carry
        lax.fori_loop(1, DP, go, 0)
        args[1][d] = src[bi_s[d, 0]]

    def down_grads():
        scale_all(0)

        def go(j, carry):
            turned = jnp.transpose(scaled[0, j].astype(F32)).astype(BF)
            for k in (0, 1):
                b = 2 * j + k
                grads[b] = dot(turned[k * R:(k + 1) * R], tok[rows_of(b), :], 1, 0).astype(BF)
            return carry

        lax.fori_loop(0, NZ, go, 0)
        send_grads(grads, gs)

    def up_grads():
        scale_all(1)

        def go(j, carry):
            mine = scaled[1, j]
            turned = jnp.transpose(mine.astype(F32)).astype(BF)
            ups = jnp.concatenate([urecv[owner_of(2 * j)], urecv[owner_of(2 * j + 1)]], axis=0)
            for k in (0, 1):
                b = 2 * j + k
                hgrads[b] = dot(turned[k * R:(k + 1) * R], cotf[z, rows_of(b), :], 1, 0).astype(BF)
                only = jnp.where((lanes >= R) if k else (lanes < R), mine, jnp.zeros((), BF))
                lorav[rows_of(b), :] = dot(only, ups, 1, 0).astype(BF)
            return carry

        lax.fori_loop(0, NZ, go, 0)
        send_grads(hgrads, hs)

    def base_chunk(cc):
        rows = rows_of(cc, CH)
        part = dot(tok[rows, :], w[...], 1, 0)
        for k in range(NZ):
            base[k, rows, :] = part[:, k * HEAD:(k + 1) * HEAD].astype(BF)

    def tig_out(cc):
        rows = rows_of(cc, CH)
        return pltpu.make_async_copy(tigv.at[rows], tig_o.at[rows], out_sem.at[cc])

    def tig_chunk(cc):
        rows = rows_of(cc, CH)
        full = jnp.concatenate([cotf[k, rows, :] for k in range(NZ)], axis=1)
        part = dot(full, w[...], 1, 1)
        mine = scaled[0, cc]
        dns = jnp.concatenate([drecv[owner_of(2 * cc)], drecv[owner_of(2 * cc + 1)]], axis=0)
        zero = jnp.zeros((), BF)
        both = jnp.concatenate([jnp.where(lanes < R, mine, zero), jnp.where(lanes >= R, mine, zero)], axis=0)
        lora = dot(both, dns, 1, 0).astype(BF).astype(F32)
        tigv[rows, :] = (part + lora).astype(BF)
        tig_out(cc).start()

    def rs(n, h, cc, dirn):
        rows = rows_of(cc, CH)
        if dirn == 0:
            dest, to = (z + h) % NZ, right
        else:
            dest, to = (z - h + NZ) % NZ, left
        return pltpu.make_async_remote_copy(
            src_ref=base.at[dest, rows], dst_ref=rsr.at[dirn, n], send_sem=rs_s.at[dirn, n],
            recv_sem=rs_r.at[dirn, n], device_id=(d, to), device_id_type=MESH)

    def rs_add(n_in, h, cc, dirn):
        rs(n_in, h, cc, dirn).wait_recv()
        dest = (z + h) % NZ if dirn == 0 else (z - h + NZ) % NZ
        rows = rows_of(cc, CH)
        base[dest, rows, :] = (base[dest, rows, :].astype(F32) + rsr[dirn, n_in].astype(F32)).astype(BF)

    def ag_step(m):
        for dirn in (0, 1):
            lag = NC - (m // (3 * NC)) * (NC // 2) * dirn

            @pl.when(m >= NC)
            def _():
                ag(m - lag, dirn).wait_recv()
            ag(m - DEPTH, dirn).wait_send()
            ag(m, dirn).start()

    def rs_step(n):
        @pl.when(n < 4)
        def _():
            for dirn in (0, 1):
                ag(MSG - DEPTH + n, dirn).wait_send()
                rs(n, 4, n + dirn * 4, dirn).start()

        @pl.when(n >= 4)
        def _():
            k, cc = (n - 4) // NC, (n - 4) % NC
            for dirn in (0, 1):
                @pl.when((k == 0) & (cc // 4 == dirn))
                def _():
                    rs_add(cc - 4 * dirn, 3, cc, dirn)

                @pl.when(k > 0)
                def _():
                    rs_add(n - NC, 3 - k, cc, dirn)
                rs(n - DEPTH, 3, cc, dirn).wait_send()
                rs(n, 3 - k, cc, dirn).start()

    def tick_a(t, carry):
        ag_step(2 * t)
        ag_step(2 * t + 1)

        @pl.when(t == T_UP)
        def _():
            back_partial()

        for k in range(8):
            @pl.when(t == T_BACK + k)
            def _():
                ar_step(0, k)

        @pl.when(t >= LAST - NC)
        def _():
            base_chunk(t - (LAST - NC))
        return carry

    lax.fori_loop(DEPTH // 2, LAST, tick_a, 0)
    ar_step(0, 8)
    down_grads()

    def ag_rest(m, carry):
        ag(m, 0).wait_recv()
        ag(m - NC // 2 + (m // (3 * NC)) * (NC // 2), 1).wait_recv()
        return carry

    def tick_b(t, carry):
        rs_step(2 * (t - LAST))
        rs_step(2 * (t - LAST) + 1)

        @pl.when(t == LAST + 1)
        def _():
            lax.fori_loop(MSG - NC, MSG, ag_rest, 0)

        @pl.when(t == T_DOWN)
        def _():
            low_partial()

        for k in range(9):
            @pl.when(t == T_LOW + k)
            def _():
                ar_step(1, k)

        @pl.when((t > T_DOWN) & (t <= T_DOWN + NC))
        def _():
            tig_chunk(t - T_DOWN - 1)

        @pl.when(t == T_LOW + 8)
        def _():
            up_grads()
        return carry

    lax.fori_loop(LAST, 2 * LAST, tick_b, 0)

    def finish(cc, carry):
        n = MSG - NC + cc
        rows = rows_of(cc, CH)
        for dirn in (0, 1):
            rs(n, 1, cc, dirn).wait_recv()
        whole = base[z, rows, :].astype(F32) + rsr[0, n].astype(F32) + rsr[1, n].astype(F32)
        valv[rows, :] = (whole + lorav[rows, :].astype(F32)).astype(BF)
        return carry

    lax.fori_loop(0, NC, finish, 0)
    cp_val = pltpu.make_async_copy(valv, val_o, out_sem.at[NC])
    cp_val.start()

    def tally(recv, acc, rows, width):
        def tile(r, carry):
            here = pl.ds(pl.multiple_of(r * rows, rows), rows)

            def add(s, sums):
                tag = tag_s[s, 0]
                piece = recv[s, here, :].astype(F32)
                return tuple(
                    sums[l] + jnp.where(tag == l + 1, piece, 0.0) for l in range(OWN))

            zero = jnp.zeros((rows, width), F32)
            sums = lax.fori_loop(0, DP, add, (zero,) * OWN)
            for l in range(OWN):
                acc[l, here, :] = sums[l]
            return carry
        lax.fori_loop(0, R // rows, tile, 0)

    x_recv(*gs)
    tally(grecv, dacc, 16, FEAT)
    cp_dm = pltpu.make_async_copy(dacc, dmg_o, out_sem.at[NC + 1])
    cp_dm.start()
    x_recv(*hs)
    tally(hrecv, uacc, 64, HEAD)
    cp_um = pltpu.make_async_copy(uacc, umg_o, out_sem.at[NC + 2])
    cp_um.start()

    def rs_rest(n, carry):
        for dirn in (0, 1):
            rs(n, 3, 0, dirn).wait_send()
        return carry

    lax.fori_loop(MSG - DEPTH, MSG, rs_rest, 0)
    for args in (tg, us, ds, gs, hs):
        x_sent(*args)
    for q in (0, 1):
        for k in range(8):
            for dirn in (0, 1):
                ar_msg(q, k, dirn).wait_send()

    def tig_rest(cc, carry):
        tig_out(cc).wait()
        return carry

    lax.fori_loop(0, NC, tig_rest, 0)
    cp_val.wait()
    cp_dm.wait()
    cp_um.wait()


def on_device(tokens, cotangent, base_weight, adapter_down, adapter_up, block_adapter, adapter_slot, adapter_rank):
    vm, dma = pltpu.VMEM, pltpu.SemaphoreType.DMA
    smem = pl.BlockSpec(memory_space=pltpu.SMEM)
    vmem = pl.BlockSpec(memory_space=pltpu.VMEM)
    hbm = pl.BlockSpec(memory_space=pl.ANY)
    scratch = [
        vm((ROWS, FEAT), BF), vm((NZ, ROWS, HEAD), BF), vm((FEAT, NZ * HEAD), BF),
        vm((OWN, R, FEAT), F32), vm((OWN, R, HEAD), F32), vm((OWN, R, FEAT), BF), vm((OWN, R, HEAD), BF),
        vm((NZ, ROWS, HEAD), BF), vm((2, MSG, CH, HEAD), BF),
        vm((DP, 8, 128), I32), vm((DP, 8, 128), I32), vm((DP, 128), I32), vm((DP, 128), I32), vm((8, 128), F32),
        vm((DP, R, HEAD), BF), vm((DP, R, HEAD), BF),
        vm((DP, R, FEAT), BF), vm((DP, R, FEAT), BF),
        vm((DP, R, FEAT), BF), vm((DP, R, FEAT), BF),
        vm((DP, R, HEAD), BF), vm((DP, R, HEAD), BF),
        vm((NB, R, FEAT), BF), vm((NB, R, HEAD), BF),
        vm((2, NZ, BLK, 2 * R), BF), vm((2, 2, 4, BLK, 2 * R), BF), vm((2, NZ, BLK, 2 * R), BF), vm((2, NZ, BLK, 2 * R), BF),
        vm((ROWS, HEAD), BF), vm((ROWS, HEAD), BF), vm((ROWS, FEAT), BF),
        vm((OWN, R, FEAT), F32), vm((OWN, R, HEAD), F32),
        pltpu.SMEM((DP, 128), I32), pltpu.SMEM((DP, 128), I32),
        dma((5,)), dma((NC + 3,)),
        dma((2, MSG)), dma((2, MSG)), dma((2, MSG)), dma((2, MSG)),
        dma((2, 2, 8)), dma((2, 2, 8)),
        dma((DP,)), dma((DP,)), dma((DP,)), dma((DP,)), dma((DP,)), dma((DP,)),
        dma((DP,)), dma((DP,)), dma((DP,)), dma((DP,)), dma((2,)),
    ]
    val, tig, dmg, umg = pl.pallas_call(
        kernel,
        out_shape=(
            jax.ShapeDtypeStruct((ROWS, HEAD), BF),
            jax.ShapeDtypeStruct((ROWS, FEAT), BF),
            jax.ShapeDtypeStruct((OWN, R, FEAT), F32),
            jax.ShapeDtypeStruct((OWN, R, HEAD), F32),
        ),
        in_specs=[smem, smem, smem, vmem, vmem, hbm, hbm, hbm, hbm, hbm],
        out_specs=(hbm, hbm, hbm, hbm),
        scratch_shapes=scratch,
        compiler_params=pltpu.CompilerParams(
            collective_id=0, has_side_effects=True, vmem_limit_bytes=54 * 2**20),
    )(
        block_adapter, adapter_slot, adapter_rank,
        adapter_slot.reshape(1, -1), adapter_rank.reshape(1, -1),
        tokens, cotangent, base_weight, jnp.swapaxes(adapter_down, 1, 2), adapter_up,
    )
    return val, tig, jnp.swapaxes(dmg, 1, 2), umg


def solution(mesh):
    return jax.shard_map(
        on_device,
        mesh=mesh,
        in_specs=(
            P("dp", "tensor"), P("dp", "tensor"), P("tensor", None), P("dp", "tensor", None),
            P("dp", None, "tensor"), P("dp"), P(), P(),
        ),
        out_specs=(P("dp", "tensor"), P("dp", "tensor"), P("dp", "tensor", None), P("dp", None, "tensor")),
        check_vma=False,
    )
```

```python
import functools

import jax
import jax.numpy as jnp
from jax import lax
from jax.experimental import pallas as pl
from jax.experimental.pallas import tpu as pltpu
from jax.sharding import PartitionSpec as P

MESH = pl.DeviceIdType.MESH
BF, F32, I32 = jnp.bfloat16, jnp.float32, jnp.int32
DP, NZ = 32, 8
ROWS, FEAT, HEAD, R, BLK, NB, OWN = 2048, 640, 128, 64, 128, 16, 4
CH = 256
NC = ROWS // CH
MSG = 3 * NC + NC // 2
DEPTH = 4
LAST = MSG // 2
T_UP = 5
T_BACK = T_UP + 1
T_HAND = 6
T_DOWN = 15
T_LOW = T_DOWN + 1
T_TALLY = 22


def dot(a, b, ca, cb):
    return lax.dot_general(a, b, (((ca,), (cb,)), ((), ())), preferred_element_type=F32)


def kernel(
    ba_s, slot_s, rank_s, slot_v, rank_v, tok_h, cot_h, w_h, dn_h, up_h,
    val_o, tig_o, dmg_o, umg_o,
    tok, cotf, w, dnf, upf, dnb, upb, base, rsr, reqs, tagr, tag_v, bi_v, scale,
    umid, usend, urecv, dmid, dsend, drecv, grads, gsend, grecv, gmid, gpart, hgrads, hsend, hrecv, hmid, hpart,
    arp, arr, tot, scaled, lorav, valv, tigv, dacc, uacc, tag_s, bi_s,
    in_sem, out_sem, ag_s, ag_r, rs_s, rs_r, ar_s, ar_r, row_s, row_r, line_s, line_r, sm_sem,
):
    d = lax.axis_index("dp")
    z = lax.axis_index("tensor")
    x, y, c = d // 8, (d // 2) % 4, d % 2
    right, left = (z + 1) % NZ, (z + NZ - 1) % NZ

    cp_cot = pltpu.make_async_copy(cot_h, cotf.at[z], in_sem.at[0])
    cp_up = pltpu.make_async_copy(up_h, upf, in_sem.at[1])
    cp_dn = pltpu.make_async_copy(dn_h, dnf, in_sem.at[2])
    cp_tok = pltpu.make_async_copy(tok_h, tok, in_sem.at[3])
    cp_w = pltpu.make_async_copy(w_h, w, in_sem.at[4])
    for cp in (cp_cot, cp_up, cp_dn, cp_tok, cp_w):
        cp.start()

    barrier = pltpu.get_barrier_semaphore()

    def at(px, py, pc):
        return px * 8 + py * 2 + pc

    def beyond(hf, k2):
        ahead, core = k2 // 2, (c + k2 % 2) % 2
        if hf == 0:
            pos = (x + ahead) % 4
            return pos * 2 + core, at(pos, y, core)
        pos = (y + ahead) % 4
        return pos * 2 + core, at(x, pos, core)

    def greet(k2, carry):
        for hf in (0, 1):
            pl.semaphore_signal(barrier, inc=1, device_id=(beyond(hf, k2)[1], z), device_id_type=MESH)
        return carry

    for to in (right, left):
        pl.semaphore_signal(barrier, inc=1, device_id=(d, to), device_id_type=MESH)
    lax.fori_loop(1, 8, greet, 0)

    pair2 = lax.broadcasted_iota(I32, (8, 128), 0)
    lane2 = lax.broadcasted_iota(I32, (8, 128), 1)
    tags = jnp.zeros((8, 128), I32)
    which = jnp.zeros((8, 128), I32)
    ranks = jnp.ones((8, 128), I32)
    for b in range(NB):
        a = ba_s[b]
        s = slot_s[a]
        o = s // OWN
        tags = jnp.where(lane2 == o, s - o * OWN + 1, tags)
        which = jnp.where(lane2 == o, b, which)
        here = (pair2 == b // 2) & ((lane2 >= R) if b % 2 else (lane2 < R))
        ranks = jnp.where(here, rank_s[a], ranks)
    reqs[...] = tags
    bi_v[...] = which
    scale[...] = R / (4.0 * ranks.astype(F32))
    cp_bi = pltpu.make_async_copy(bi_v, bi_s, sm_sem.at[0])
    cp_bi.start()
    pl.semaphore_wait(barrier, 16)

    def ag(m, dirn):
        h, cc = m // NC, m % NC
        row = cc * CH
        if dirn == 0:
            shard, to = (z - h + NZ) % NZ, right
        else:
            shard, to = (z + h) % NZ, left
            row = row + (h // 3) * (ROWS // 2)
        part = cotf.at[shard, pl.ds(pl.multiple_of(row, CH), CH)]
        return pltpu.make_async_remote_copy(
            src_ref=part, dst_ref=part, send_sem=ag_s.at[dirn, m], recv_sem=ag_r.at[dirn, m],
            device_id=(d, to), device_id_type=MESH)

    cp_cot.wait()

    def ag_first(m, carry):
        ag(m, 0).start()
        ag(m, 1).start()
        return carry

    lax.fori_loop(0, DEPTH, ag_first, 0)

    along = (y, x)
    across = (x, y)
    me8 = tuple(q * 2 + c for q in across)

    def owner(hf, p, q, core):
        return at(q, p, core) if hf == 0 else at(p, q, core)

    def row_copy(e, hf, k2, src, dst):
        return pltpu.make_async_remote_copy(
            src_ref=src, dst_ref=dst, send_sem=row_s.at[e, hf, k2], recv_sem=row_r.at[e, hf, k2],
            device_id=(beyond(hf, k2)[1], z), device_id_type=MESH)

    def line_copy(e, hf, k, src, dst):
        to = at(x, (y + k) % 4, c) if hf == 0 else at((x + k) % 4, y, c)
        return pltpu.make_async_remote_copy(
            src_ref=src, dst_ref=dst, send_sem=line_s.at[e, hf, k], recv_sem=line_r.at[e, hf, k],
            device_id=(to, z), device_id_type=MESH)

    TAG, UP, DOWN, GRAD, HGRAD = 0, 1, 2, 3, 4

    def row_msg(e, hf, k2):
        if e == TAG:
            return row_copy(e, hf, k2, reqs, tagr.at[hf, me8[hf]])
        g = beyond(hf, k2)[0]
        if e in (UP, DOWN):
            src, dst = ((usend, urecv), (dsend, drecv))[e - UP]
            return row_copy(e, hf, k2, src.at[hf, g], dst.at[hf, pl.ds(me8[hf] * 4, 4)])
        src, dst = ((gsend, grecv), (hsend, hrecv))[e - GRAD]
        return row_copy(e, hf, k2, src.at[hf, g], dst.at[hf, me8[hf]])

    def line_msg(e, hf, k):
        p = along[hf]
        if e in (UP, DOWN):
            src, dst = ((upb, umid), (dnb, dmid))[e - UP]
            return line_copy(e, hf, k, src.at[hf], dst.at[hf, p])
        src, dst = ((gmid, gpart), (hmid, hpart))[e - GRAD]
        return line_copy(e, hf, k, src.at[hf, (p + k) % 4], dst.at[hf, p])

    def each_row(e, what):
        def go(j, carry):
            k2 = (j * 3) % 8
            for hf in (0, 1):
                what(row_msg(e, hf, k2), hf, k2)
            return carry
        lax.fori_loop(1, 8, go, 0)

    def each_line(e, what):
        for k in (1, 3, 2):
            for hf in (0, 1):
                what(line_msg(e, hf, k))

    def row_arrived(e):
        each_row(e, lambda copy, hf, k2: copy.wait_recv())

    def line_arrived(e):
        each_line(e, lambda copy: copy.wait_recv())

    each_row(TAG, lambda copy, hf, k2: copy.start())
    for hf in (0, 1):
        tagr[hf, me8[hf]] = reqs[...]

    cp_up.wait()
    cp_dn.wait()
    RH = R // 2
    for l in range(OWN):
        mine = slot_v[...] == d * OWN + l
        rank = jnp.sum(jnp.where(mine, rank_v[...], 0), axis=1, keepdims=True)
        for hf in (0, 1):
            rows = slice(hf * RH, (hf + 1) * RH)
            keep = lax.broadcasted_iota(I32, (RH, HEAD), 0) + hf * RH < rank
            upb[hf, l] = jnp.where(keep, upf[l, rows, :], 0.0).astype(BF)
    each_line(UP, lambda copy: copy.start())
    for l in range(OWN):
        mine = slot_v[...] == d * OWN + l
        rank = jnp.sum(jnp.where(mine, rank_v[...], 0), axis=1, keepdims=True)
        for hf in (0, 1):
            rows = slice(hf * RH, (hf + 1) * RH)
            keep = lax.broadcasted_iota(I32, (RH, FEAT), 0) + hf * RH < rank
            dnb[hf, l] = jnp.where(keep, dnf[l, rows, :], 0.0).astype(BF)
    each_line(DOWN, lambda copy: copy.start())
    for hf in (0, 1):
        umid[hf, along[hf]] = upb[hf]
        dmid[hf, along[hf]] = dnb[hf]
    row_arrived(TAG)
    for hf in (0, 1):
        tag_v[hf] = tagr[hf, :, 0, :]
    cp_tag = pltpu.make_async_copy(tag_v, tag_s, sm_sem.at[1])
    cp_tag.start()
    cp_tag.wait()

    def wanted(hf, g, p):
        return tag_s[hf, g, owner(hf, p, across[hf], c)]

    def hand_on(e, mid, send, recv):
        line_arrived(e)

        def go(copy, hf, k2):
            g = beyond(hf, k2)[0]
            for p in range(4):
                send[hf, g, p] = mid[hf, p, jnp.maximum(wanted(hf, g, p) - 1, 0)]
            copy.start()

        each_row(e, go)
        for hf in (0, 1):
            for p in range(4):
                recv[hf, me8[hf] * 4 + p] = mid[hf, p, jnp.maximum(wanted(hf, me8[hf], p) - 1, 0)]

    hand_on(UP, umid, usend, urecv)
    cp_bi.wait()
    cp_tok.wait()
    cp_w.wait()

    def of_block(recv, b):
        o = slot_s[ba_s[b]] // OWN
        ox, oy, oc = o // 8, (o // 2) % 4, o % 2
        return [recv[0, (ox * 2 + oc) * 4 + oy], recv[1, (oy * 2 + oc) * 4 + ox]]

    def of_blocks(recv, *bs):
        return jnp.concatenate([part for b in bs for part in of_block(recv, b)], axis=0)

    half = (slice(0, BLK // 2), slice(BLK // 2, BLK))

    def ar_copy(q, k, dirn, src, dst):
        return pltpu.make_async_remote_copy(
            src_ref=src, dst_ref=dst, send_sem=ar_s.at[q, dirn, k], recv_sem=ar_r.at[q, dirn, k],
            device_id=(d, (right, left)[dirn]), device_id_type=MESH)

    def ar_msg(q, k, dirn):
        sgn = (1, -1)[dirn]
        if k == 0:
            p = (z + 4) % NZ
            lo = (0, BLK // 2)[dirn]
            return ar_copy(q, k, dirn, arp.at[q, p, pl.ds(lo, BLK // 2)], arr.at[q, dirn, 0, pl.ds(lo, BLK // 2)])
        if k < 4:
            p = (z + sgn * (4 - k) + NZ) % NZ
            return ar_copy(q, k, dirn, arp.at[q, p], arr.at[q, dirn, k])
        p = (z - sgn * (k - 4) + NZ) % NZ
        if k < 7:
            return ar_copy(q, k, dirn, tot.at[q, p], tot.at[q, p])
        lo = (0, BLK // 2)[dirn]
        part = tot.at[q, p, pl.ds(lo, BLK // 2)]
        return ar_copy(q, k, dirn, part, part)

    def ar_step(q, k):
        if k > 0:
            for dirn in (0, 1):
                ar_msg(q, k - 1, dirn).wait_recv()
        if k in (1, 2, 3):
            for dirn in (0, 1):
                p = (z + (1, -1)[dirn] * (4 - k) + NZ) % NZ
                rows = half[dirn] if k == 1 else slice(0, BLK)
                arp[q, p, rows] = (arp[q, p, rows].astype(F32) + arr[q, dirn, k - 1, rows].astype(F32)).astype(BF)
        if k == 4:
            tot[q, z] = (arp[q, z].astype(F32) + arr[q, 0, 3].astype(F32) + arr[q, 1, 3].astype(F32)).astype(BF)
        if k < 8:
            for dirn in (0, 1):
                ar_msg(q, k, dirn).start()

    def scale_all(q):
        def go(j, carry):
            scaled[q, j] = (scale[pl.ds(j, 1), :] * tot[q, j].astype(F32)).astype(BF)
            return carry
        lax.fori_loop(0, NZ, go, 0)

    lanes = lax.broadcasted_iota(I32, (BLK, 2 * R), 1)

    def rows_of(b, n=BLK):
        return pl.ds(pl.multiple_of(b * n, n), n)

    def low_rank(e, q, recv, data):
        row_arrived(e)

        def go(j, carry):
            parts = [dot(data(2 * j + k), of_blocks(recv, 2 * j + k), 1, 1) for k in (0, 1)]
            arp[q, j] = jnp.concatenate(parts, axis=1).astype(BF)
            return carry

        lax.fori_loop(0, NZ, go, 0)

    def tok_of(b):
        return tok[rows_of(b), :]

    def cot_of(b):
        return cotf[z, rows_of(b), :]

    def send_grads(e, src, send, recv):
        def pick(hf, q, core, p):
            return src[hf, bi_s[0, owner(hf, p, q, core)]]

        def go(copy, hf, k2):
            g = beyond(hf, k2)[0]
            for p in range(4):
                send[hf, g, p] = pick(hf, g // 2, g % 2, p)
            copy.start()

        each_row(e, go)
        for hf in (0, 1):
            for p in range(4):
                recv[hf, me8[hf], p] = pick(hf, across[hf], c, p)

    def tally(e, recv, mid, part, rows, width):
        row_arrived(e)
        for hf in (0, 1):
            def tile(i, carry):
                p, r = i // (RH // rows), i % (RH // rows)
                here = pl.ds(pl.multiple_of(r * rows, rows), rows)

                def add(g, sums):
                    tag = wanted(hf, g, p)
                    piece = recv[hf, g, p, here, :].astype(F32)
                    return tuple(
                        sums[l] + jnp.where(tag == l + 1, piece, 0.0) for l in range(OWN))

                zero = jnp.zeros((rows, width), F32)
                sums = lax.fori_loop(0, 8, add, (zero,) * OWN)
                for l in range(OWN):
                    mid[hf, p, l, here, :] = sums[l].astype(BF)
                return carry
            lax.fori_loop(0, 4 * (RH // rows), tile, 0)
        each_line(e, lambda copy: copy.start())
        for hf in (0, 1):
            part[hf, along[hf]] = mid[hf, along[hf]]

    def total(e, part, acc):
        line_arrived(e)
        for hf in (0, 1):
            rows = slice(hf * RH, (hf + 1) * RH)
            for l in range(OWN):
                acc[l, rows, :] = sum(part[hf, p, l].astype(F32) for p in range(4))

    def down_grads():
        scale_all(0)

        def go(j, carry):
            turned = jnp.transpose(scaled[0, j].astype(F32)).astype(BF)
            for k in (0, 1):
                b = 2 * j + k
                piece = dot(turned[k * R:(k + 1) * R], tok_of(b), 1, 0).astype(BF)
                for hf in (0, 1):
                    grads[hf, b] = piece[hf * RH:(hf + 1) * RH]
            return carry

        lax.fori_loop(0, NZ, go, 0)
        send_grads(GRAD, grads, gsend, grecv)

    def up_grads():
        scale_all(1)

        def go(j, carry):
            mine = scaled[1, j]
            turned = jnp.transpose(mine.astype(F32)).astype(BF)
            ups = of_blocks(urecv, 2 * j, 2 * j + 1)
            for k in (0, 1):
                b = 2 * j + k
                piece = dot(turned[k * R:(k + 1) * R], cot_of(b), 1, 0).astype(BF)
                for hf in (0, 1):
                    hgrads[hf, b] = piece[hf * RH:(hf + 1) * RH]
                only = jnp.where((lanes >= R) if k else (lanes < R), mine, jnp.zeros((), BF))
                lorav[rows_of(b), :] = dot(only, ups, 1, 0).astype(BF)
            return carry

        lax.fori_loop(0, NZ, go, 0)
        send_grads(HGRAD, hgrads, hsend, hrecv)

    def base_chunk(cc):
        rows = rows_of(cc, CH)
        part = dot(tok[rows, :], w[...], 1, 0)
        for k in range(NZ):
            base[k, rows, :] = part[:, k * HEAD:(k + 1) * HEAD].astype(BF)

    def tig_out(cc):
        rows = rows_of(cc, CH)
        return pltpu.make_async_copy(tigv.at[rows], tig_o.at[rows], out_sem.at[cc])

    def tig_chunk(cc):
        rows = rows_of(cc, CH)
        full = jnp.concatenate([cotf[k, rows, :] for k in range(NZ)], axis=1)
        part = dot(full, w[...], 1, 1)
        mine = scaled[0, cc]
        zero = jnp.zeros((), BF)
        both = jnp.concatenate([jnp.where(lanes < R, mine, zero), jnp.where(lanes >= R, mine, zero)], axis=0)
        lora = dot(both, of_blocks(drecv, 2 * cc, 2 * cc + 1), 1, 0).astype(BF).astype(F32)
        tigv[rows, :] = (part + lora).astype(BF)
        tig_out(cc).start()

    def rs(n, h, cc, dirn):
        rows = rows_of(cc, CH)
        if dirn == 0:
            dest, to = (z + h) % NZ, right
        else:
            dest, to = (z - h + NZ) % NZ, left
        return pltpu.make_async_remote_copy(
            src_ref=base.at[dest, rows], dst_ref=rsr.at[dirn, n], send_sem=rs_s.at[dirn, n],
            recv_sem=rs_r.at[dirn, n], device_id=(d, to), device_id_type=MESH)

    def rs_add(n_in, h, cc, dirn):
        rs(n_in, h, cc, dirn).wait_recv()
        dest = (z + h) % NZ if dirn == 0 else (z - h + NZ) % NZ
        rows = rows_of(cc, CH)
        base[dest, rows, :] = (base[dest, rows, :].astype(F32) + rsr[dirn, n_in].astype(F32)).astype(BF)

    def ag_step(m):
        for dirn in (0, 1):
            lag = NC - (m // (3 * NC)) * (NC // 2) * dirn

            @pl.when(m >= NC)
            def _():
                ag(m - lag, dirn).wait_recv()
            ag(m - DEPTH, dirn).wait_send()
            ag(m, dirn).start()

    def rs_step(n):
        @pl.when(n < 4)
        def _():
            for dirn in (0, 1):
                ag(MSG - DEPTH + n, dirn).wait_send()
                rs(n, 4, n + dirn * 4, dirn).start()

        @pl.when(n >= 4)
        def _():
            k, cc = (n - 4) // NC, (n - 4) % NC
            for dirn in (0, 1):
                @pl.when((k == 0) & (cc // 4 == dirn))
                def _():
                    rs_add(cc - 4 * dirn, 3, cc, dirn)

                @pl.when(k > 0)
                def _():
                    rs_add(n - NC, 3 - k, cc, dirn)
                rs(n - DEPTH, 3, cc, dirn).wait_send()
                rs(n, 3 - k, cc, dirn).start()

    def tick_a(t, carry):
        ag_step(2 * t)
        ag_step(2 * t + 1)

        @pl.when(t == T_UP)
        def _():
            low_rank(UP, 0, urecv, cot_of)

        for k in range(8):
            @pl.when(t == T_BACK + k)
            def _():
                ar_step(0, k)

        @pl.when(t == T_HAND)
        def _():
            hand_on(DOWN, dmid, dsend, drecv)

        @pl.when(t >= LAST - NC)
        def _():
            base_chunk(t - (LAST - NC))
        return carry

    lax.fori_loop(DEPTH // 2, LAST, tick_a, 0)
    ar_step(0, 8)
    down_grads()

    def ag_rest(m, carry):
        ag(m, 0).wait_recv()
        ag(m - NC // 2 + (m // (3 * NC)) * (NC // 2), 1).wait_recv()
        return carry

    def tick_b(t, carry):
        rs_step(2 * (t - LAST))
        rs_step(2 * (t - LAST) + 1)

        @pl.when(t == LAST + 1)
        def _():
            lax.fori_loop(MSG - NC, MSG, ag_rest, 0)

        @pl.when(t == T_DOWN)
        def _():
            low_rank(DOWN, 1, drecv, tok_of)

        for k in range(9):
            @pl.when(t == T_LOW + k)
            def _():
                ar_step(1, k)

        @pl.when((t > T_DOWN) & (t <= T_DOWN + NC))
        def _():
            tig_chunk(t - T_DOWN - 1)

        @pl.when(t == T_TALLY)
        def _():
            tally(GRAD, grecv, gmid, gpart, 16, FEAT)

        @pl.when(t == T_LOW + 8)
        def _():
            up_grads()

        @pl.when(t == T_LOW + 10)
        def _():
            tally(HGRAD, hrecv, hmid, hpart, 32, HEAD)
        return carry

    lax.fori_loop(LAST, 2 * LAST, tick_b, 0)

    def finish(cc, carry):
        n = MSG - NC + cc
        rows = rows_of(cc, CH)
        for dirn in (0, 1):
            rs(n, 1, cc, dirn).wait_recv()
        whole = base[z, rows, :].astype(F32) + rsr[0, n].astype(F32) + rsr[1, n].astype(F32)
        valv[rows, :] = (whole + lorav[rows, :].astype(F32)).astype(BF)
        return carry

    total(GRAD, gpart, dacc)
    cp_dm = pltpu.make_async_copy(dacc, dmg_o, out_sem.at[NC + 1])
    cp_dm.start()
    lax.fori_loop(0, NC, finish, 0)
    cp_val = pltpu.make_async_copy(valv, val_o, out_sem.at[NC])
    cp_val.start()
    total(HGRAD, hpart, uacc)
    cp_um = pltpu.make_async_copy(uacc, umg_o, out_sem.at[NC + 2])
    cp_um.start()

    def rs_rest(n, carry):
        for dirn in (0, 1):
            rs(n, 3, 0, dirn).wait_send()
        return carry

    lax.fori_loop(MSG - DEPTH, MSG, rs_rest, 0)
    for e in (TAG, UP, DOWN, GRAD, HGRAD):
        each_row(e, lambda copy, hf, k2: copy.wait_send())
        if e != TAG:
            each_line(e, lambda copy: copy.wait_send())
    for q in (0, 1):
        for k in range(8):
            for dirn in (0, 1):
                ar_msg(q, k, dirn).wait_send()

    def tig_rest(cc, carry):
        tig_out(cc).wait()
        return carry

    lax.fori_loop(0, NC, tig_rest, 0)
    cp_val.wait()
    cp_dm.wait()
    cp_um.wait()


def on_device(tokens, cotangent, base_weight, adapter_down, adapter_up, block_adapter, adapter_slot, adapter_rank):
    vm, dma = pltpu.VMEM, pltpu.SemaphoreType.DMA
    smem = pl.BlockSpec(memory_space=pltpu.SMEM)
    vmem = pl.BlockSpec(memory_space=pltpu.VMEM)
    hbm = pl.BlockSpec(memory_space=pl.ANY)
    rh = R // 2
    scratch = [
        vm((ROWS, FEAT), BF), vm((NZ, ROWS, HEAD), BF), vm((FEAT, NZ * HEAD), BF),
        vm((OWN, R, FEAT), F32), vm((OWN, R, HEAD), F32), vm((2, OWN, rh, FEAT), BF), vm((2, OWN, rh, HEAD), BF),
        vm((NZ, ROWS, HEAD), BF), vm((2, MSG, CH, HEAD), BF),
        vm((8, 128), I32), vm((2, 8, 8, 128), I32), vm((2, 8, 128), I32), vm((8, 128), I32), vm((8, 128), F32),
        vm((2, 4, OWN, rh, HEAD), BF), vm((2, 8, 4, rh, HEAD), BF), vm((2, DP, rh, HEAD), BF),
        vm((2, 4, OWN, rh, FEAT), BF), vm((2, 8, 4, rh, FEAT), BF), vm((2, DP, rh, FEAT), BF),
        vm((2, NB, rh, FEAT), BF), vm((2, 8, 4, rh, FEAT), BF), vm((2, 8, 4, rh, FEAT), BF),
        vm((2, 4, OWN, rh, FEAT), BF), vm((2, 4, OWN, rh, FEAT), BF),
        vm((2, NB, rh, HEAD), BF), vm((2, 8, 4, rh, HEAD), BF), vm((2, 8, 4, rh, HEAD), BF),
        vm((2, 4, OWN, rh, HEAD), BF), vm((2, 4, OWN, rh, HEAD), BF),
        vm((2, NZ, BLK, 2 * R), BF), vm((2, 2, 4, BLK, 2 * R), BF), vm((2, NZ, BLK, 2 * R), BF), vm((2, NZ, BLK, 2 * R), BF),
        vm((ROWS, HEAD), BF), vm((ROWS, HEAD), BF), vm((ROWS, FEAT), BF),
        vm((OWN, R, FEAT), F32), vm((OWN, R, HEAD), F32),
        pltpu.SMEM((2, 8, 128), I32), pltpu.SMEM((8, 128), I32),
        dma((5,)), dma((NC + 3,)),
        dma((2, MSG)), dma((2, MSG)), dma((2, MSG)), dma((2, MSG)),
        dma((2, 2, 8)), dma((2, 2, 8)),
        dma((5, 2, 8)), dma((5, 2, 8)), dma((5, 2, 4)), dma((5, 2, 4)), dma((2,)),
    ]
    val, tig, dmg, umg = pl.pallas_call(
        kernel,
        out_shape=(
            jax.ShapeDtypeStruct((ROWS, HEAD), BF),
            jax.ShapeDtypeStruct((ROWS, FEAT), BF),
            jax.ShapeDtypeStruct((OWN, R, FEAT), F32),
            jax.ShapeDtypeStruct((OWN, R, HEAD), F32),
        ),
        in_specs=[smem, smem, smem, vmem, vmem, hbm, hbm, hbm, hbm, hbm],
        out_specs=(hbm, hbm, hbm, hbm),
        scratch_shapes=scratch,
        compiler_params=pltpu.CompilerParams(
            collective_id=0, has_side_effects=True, vmem_limit_bytes=54 * 2**20),
    )(
        block_adapter, adapter_slot, adapter_rank,
        adapter_slot.reshape(1, -1), adapter_rank.reshape(1, -1),
        tokens, cotangent, base_weight, jnp.swapaxes(adapter_down, 1, 2), adapter_up,
    )
    return val, tig, jnp.swapaxes(dmg, 1, 2), umg


def solution(mesh):
    return jax.shard_map(
        on_device,
        mesh=mesh,
        in_specs=(
            P("dp", "tensor"), P("dp", "tensor"), P("tensor", None), P("dp", "tensor", None),
            P("dp", None, "tensor"), P("dp"), P(), P(),
        ),
        out_specs=(P("dp", "tensor"), P("dp", "tensor"), P("dp", "tensor", None), P("dp", None, "tensor")),
        check_vma=False,
    )
```

```python
import functools

import jax
import jax.numpy as jnp
from jax import lax
from jax.experimental import pallas as pl
from jax.experimental.pallas import tpu as pltpu
from jax.sharding import PartitionSpec as P

MESH = pl.DeviceIdType.MESH
BF, F32, I32 = jnp.bfloat16, jnp.float32, jnp.int32
DP, NZ = 32, 8
ROWS, FEAT, HEAD, R, BLK, NB, OWN = 2048, 640, 128, 64, 128, 16, 4
CH = 256
NC = ROWS // CH
MSG = 3 * NC + NC // 2
DEPTH = 3
U_BACK = 8
U_HAND = 11
U_LOW = 24
HOPS = (3, 3)
U_BACK_HOP = U_BACK + 1
U_LOW_HOP = U_LOW + 2
U_BACK_END = U_BACK_HOP + 8 * HOPS[0]
U_LOW_END = U_LOW_HOP + 8 * HOPS[1]
U_BASE = 9
U_TIG = U_BACK_END + 2
U_TALLY = 46
U_HTALLY = U_LOW_END + 4


def dot(a, b, ca, cb):
    return lax.dot_general(a, b, (((ca,), (cb,)), ((), ())), preferred_element_type=F32)


def kernel(
    ba_s, slot_s, rank_s, slot_v, rank_v, tok_h, cot_h, w_h, dn_h, up_h,
    valv, tigv, dacc, uacc,
    tok, cotf, w, dnf, upf, dnb, upb, base, rsr, reqs, tagr, tag_v, bi_v, scale,
    umid, usend, urecv, dmid, dsend, drecv, grads, gsend, grecv, gmid, gpart, hgrads, hsend, hrecv, hmid, hpart,
    arp, arr, tot, scaled, lorav, tag_s, bi_s,
    in_sem, ag_s, ag_r, rs_s, rs_r, ar_s, ar_r, row_s, row_r, line_s, line_r, sm_sem,
):
    d = lax.axis_index("dp")
    z = lax.axis_index("tensor")
    x, y, c = d // 8, (d // 2) % 4, d % 2
    right, left = (z + 1) % NZ, (z + NZ - 1) % NZ

    cp_cot = pltpu.make_async_copy(cot_h, cotf.at[z], in_sem.at[0])
    cp_up = pltpu.make_async_copy(up_h, upf, in_sem.at[1])
    cp_dn = pltpu.make_async_copy(dn_h, dnf, in_sem.at[2])
    cp_tok = pltpu.make_async_copy(tok_h, tok, in_sem.at[3])
    cp_w = pltpu.make_async_copy(w_h, w, in_sem.at[4])
    for cp in (cp_cot, cp_up, cp_dn, cp_tok, cp_w):
        cp.start()

    barrier = pltpu.get_barrier_semaphore()

    def at(px, py, pc):
        return px * 8 + py * 2 + pc

    def beyond(hf, k2):
        ahead, core = k2 // 2, (c + k2 % 2) % 2
        if hf == 0:
            pos = (x + ahead) % 4
            return pos * 2 + core, at(pos, y, core)
        pos = (y + ahead) % 4
        return pos * 2 + core, at(x, pos, core)

    def greet(k2, carry):
        for hf in (0, 1):
            pl.semaphore_signal(barrier, inc=1, device_id=(beyond(hf, k2)[1], z), device_id_type=MESH)
        return carry

    for to in (right, left):
        pl.semaphore_signal(barrier, inc=1, device_id=(d, to), device_id_type=MESH)
    lax.fori_loop(1, 8, greet, 0)

    pair2 = lax.broadcasted_iota(I32, (8, 128), 0)
    lane2 = lax.broadcasted_iota(I32, (8, 128), 1)
    tags = jnp.zeros((8, 128), I32)
    which = jnp.zeros((8, 128), I32)
    ranks = jnp.ones((8, 128), I32)
    for b in range(NB):
        a = ba_s[b]
        s = slot_s[a]
        o = s // OWN
        tags = jnp.where(lane2 == o, s - o * OWN + 1, tags)
        which = jnp.where(lane2 == o, b, which)
        here = (pair2 == b // 2) & ((lane2 >= R) if b % 2 else (lane2 < R))
        ranks = jnp.where(here, rank_s[a], ranks)
    reqs[...] = tags
    bi_v[...] = which
    scale[...] = R / (4.0 * ranks.astype(F32))
    cp_bi = pltpu.make_async_copy(bi_v, bi_s, sm_sem.at[0])
    cp_bi.start()
    pl.semaphore_wait(barrier, 16)

    def ag(m, dirn):
        h, cc = m // NC, m % NC
        row = cc * CH
        if dirn == 0:
            shard, to = (z - h + NZ) % NZ, right
        else:
            shard, to = (z + h) % NZ, left
            row = row + (h // 3) * (ROWS // 2)
        part = cotf.at[shard, pl.ds(pl.multiple_of(row, CH), CH)]
        return pltpu.make_async_remote_copy(
            src_ref=part, dst_ref=part, send_sem=ag_s.at[dirn, m], recv_sem=ag_r.at[dirn, m],
            device_id=(d, to), device_id_type=MESH)

    cp_cot.wait()

    def ag_first(m, carry):
        ag(m, 0).start()
        ag(m, 1).start()
        return carry

    lax.fori_loop(0, DEPTH, ag_first, 0)

    along = (y, x)
    across = (x, y)
    me8 = tuple(q * 2 + c for q in across)

    def owner(hf, p, q, core):
        return at(q, p, core) if hf == 0 else at(p, q, core)

    def row_copy(e, hf, k2, src, dst):
        return pltpu.make_async_remote_copy(
            src_ref=src, dst_ref=dst, send_sem=row_s.at[e, hf, k2], recv_sem=row_r.at[e, hf, k2],
            device_id=(beyond(hf, k2)[1], z), device_id_type=MESH)

    def line_copy(e, hf, k, src, dst):
        to = at(x, (y + k) % 4, c) if hf == 0 else at((x + k) % 4, y, c)
        return pltpu.make_async_remote_copy(
            src_ref=src, dst_ref=dst, send_sem=line_s.at[e, hf, k], recv_sem=line_r.at[e, hf, k],
            device_id=(to, z), device_id_type=MESH)

    TAG, UP, DOWN, GRAD, HGRAD = 0, 1, 2, 3, 4

    def row_msg(e, hf, k2):
        if e == TAG:
            return row_copy(e, hf, k2, reqs, tagr.at[hf, me8[hf]])
        g = beyond(hf, k2)[0]
        if e in (UP, DOWN):
            src, dst = ((usend, urecv), (dsend, drecv))[e - UP]
            return row_copy(e, hf, k2, src.at[hf, g], dst.at[hf, pl.ds(me8[hf] * 4, 4)])
        src, dst = ((gsend, grecv), (hsend, hrecv))[e - GRAD]
        return row_copy(e, hf, k2, src.at[hf, g], dst.at[hf, me8[hf]])

    def line_msg(e, hf, k):
        p = along[hf]
        if e in (UP, DOWN):
            src, dst = ((upb, umid), (dnb, dmid))[e - UP]
            return line_copy(e, hf, k, src.at[hf], dst.at[hf, p])
        src, dst = ((gmid, gpart), (hmid, hpart))[e - GRAD]
        return line_copy(e, hf, k, src.at[hf, (p + k) % 4], dst.at[hf, p])

    def each_row(e, what):
        def go(j, carry):
            k2 = (j * 3) % 8
            for hf in (0, 1):
                what(row_msg(e, hf, k2), hf, k2)
            return carry
        lax.fori_loop(1, 8, go, 0)

    def each_line(e, what):
        for k in (1, 3, 2):
            for hf in (0, 1):
                what(line_msg(e, hf, k))

    def row_arrived(e):
        each_row(e, lambda copy, hf, k2: copy.wait_recv())

    def line_arrived(e):
        each_line(e, lambda copy: copy.wait_recv())

    each_row(TAG, lambda copy, hf, k2: copy.start())
    for hf in (0, 1):
        tagr[hf, me8[hf]] = reqs[...]

    cp_up.wait()
    cp_dn.wait()
    RH = R // 2
    for l in range(OWN):
        mine = slot_v[...] == d * OWN + l
        rank = jnp.sum(jnp.where(mine, rank_v[...], 0), axis=1, keepdims=True)
        for hf in (0, 1):
            rows = slice(hf * RH, (hf + 1) * RH)
            keep = lax.broadcasted_iota(I32, (RH, HEAD), 0) + hf * RH < rank
            upb[hf, l] = jnp.where(keep, upf[l, rows, :], 0.0).astype(BF)
    each_line(UP, lambda copy: copy.start())
    for l in range(OWN):
        mine = slot_v[...] == d * OWN + l
        rank = jnp.sum(jnp.where(mine, rank_v[...], 0), axis=1, keepdims=True)
        for hf in (0, 1):
            rows = slice(hf * RH, (hf + 1) * RH)
            keep = lax.broadcasted_iota(I32, (RH, FEAT), 0) + hf * RH < rank
            dnb[hf, l] = jnp.where(keep, dnf[l, rows, :], 0.0).astype(BF)
    for hf in (0, 1):
        umid[hf, along[hf]] = upb[hf]
        dmid[hf, along[hf]] = dnb[hf]
    row_arrived(TAG)
    for hf in (0, 1):
        tag_v[hf] = tagr[hf, :, 0, :]
    cp_tag = pltpu.make_async_copy(tag_v, tag_s, sm_sem.at[1])
    cp_tag.start()
    cp_tag.wait()

    def wanted(hf, g, p):
        return tag_s[hf, g, owner(hf, p, across[hf], c)]

    def hand_on(e, mid, send, recv):
        line_arrived(e)

        def go(copy, hf, k2):
            g = beyond(hf, k2)[0]
            for p in range(4):
                send[hf, g, p] = mid[hf, p, jnp.maximum(wanted(hf, g, p) - 1, 0)]
            copy.start()

        each_row(e, go)
        for hf in (0, 1):
            for p in range(4):
                recv[hf, me8[hf] * 4 + p] = mid[hf, p, jnp.maximum(wanted(hf, me8[hf], p) - 1, 0)]

    hand_on(UP, umid, usend, urecv)
    each_line(DOWN, lambda copy: copy.start())
    cp_bi.wait()
    cp_tok.wait()
    cp_w.wait()

    def of_block(recv, b):
        o = slot_s[ba_s[b]] // OWN
        ox, oy, oc = o // 8, (o // 2) % 4, o % 2
        return [recv[0, (ox * 2 + oc) * 4 + oy], recv[1, (oy * 2 + oc) * 4 + ox]]

    def of_blocks(recv, *bs):
        return jnp.concatenate([part for b in bs for part in of_block(recv, b)], axis=0)

    half = (slice(0, BLK // 2), slice(BLK // 2, BLK))

    def ar_copy(q, k, dirn, src, dst):
        return pltpu.make_async_remote_copy(
            src_ref=src, dst_ref=dst, send_sem=ar_s.at[q, dirn, k], recv_sem=ar_r.at[q, dirn, k],
            device_id=(d, (right, left)[dirn]), device_id_type=MESH)

    def ar_msg(q, k, dirn):
        sgn = (1, -1)[dirn]
        if k == 0:
            p = (z + 4) % NZ
            lo = (0, BLK // 2)[dirn]
            return ar_copy(q, k, dirn, arp.at[q, p, pl.ds(lo, BLK // 2)], arr.at[q, dirn, 0, pl.ds(lo, BLK // 2)])
        if k < 4:
            p = (z + sgn * (4 - k) + NZ) % NZ
            return ar_copy(q, k, dirn, arp.at[q, p], arr.at[q, dirn, k])
        p = (z - sgn * (k - 4) + NZ) % NZ
        if k < 7:
            return ar_copy(q, k, dirn, tot.at[q, p], tot.at[q, p])
        lo = (0, BLK // 2)[dirn]
        part = tot.at[q, p, pl.ds(lo, BLK // 2)]
        return ar_copy(q, k, dirn, part, part)

    def ar_step(q, k):
        if k > 0:
            for dirn in (0, 1):
                ar_msg(q, k - 1, dirn).wait_recv()
        if k in (1, 2, 3):
            for dirn in (0, 1):
                p = (z + (1, -1)[dirn] * (4 - k) + NZ) % NZ
                rows = half[dirn] if k == 1 else slice(0, BLK)
                arp[q, p, rows] = (arp[q, p, rows].astype(F32) + arr[q, dirn, k - 1, rows].astype(F32)).astype(BF)
        if k == 4:
            tot[q, z] = (arp[q, z].astype(F32) + arr[q, 0, 3].astype(F32) + arr[q, 1, 3].astype(F32)).astype(BF)
        if k < 8:
            for dirn in (0, 1):
                ar_msg(q, k, dirn).start()

    def scale_all(q):
        def go(j, carry):
            scaled[q, j] = (scale[pl.ds(j, 1), :] * tot[q, j].astype(F32)).astype(BF)
            return carry
        lax.fori_loop(0, NZ, go, 0)

    lanes = lax.broadcasted_iota(I32, (BLK, 2 * R), 1)

    def rows_of(b, n=BLK):
        return pl.ds(pl.multiple_of(b * n, n), n)

    def low_rank(q, recv, data, lo, hi):
        def go(j, carry):
            parts = [dot(data(2 * j + k), of_blocks(recv, 2 * j + k), 1, 1) for k in (0, 1)]
            arp[q, j] = jnp.concatenate(parts, axis=1).astype(BF)
            return carry

        lax.fori_loop(lo, hi, go, 0)

    def tok_of(b):
        return tok[rows_of(b), :]

    def cot_of(b):
        return cotf[z, rows_of(b), :]

    def send_grads(e, src, send, recv):
        def pick(hf, q, core, p):
            return src[hf, bi_s[0, owner(hf, p, q, core)]]

        def go(copy, hf, k2):
            g = beyond(hf, k2)[0]
            for p in range(4):
                send[hf, g, p] = pick(hf, g // 2, g % 2, p)
            copy.start()

        each_row(e, go)
        for hf in (0, 1):
            for p in range(4):
                recv[hf, me8[hf], p] = pick(hf, across[hf], c, p)

    def tally(e, recv, mid, part, halves=(0, 1)):
        shape = (OWN * RH, 8 * RH)
        to, frm = lax.broadcasted_iota(I32, shape, 0), lax.broadcasted_iota(I32, shape, 1)
        same_row = (to % RH) == (frm % RH)
        slot, core = to // RH + 1, frm // RH
        for hf in halves:
            def place(p, carry):
                tags = jnp.zeros(shape, I32)
                for g in range(8):
                    tags = jnp.where(core == g, wanted(hf, g, p), tags)
                pick = jnp.where(same_row & (tags == slot), 1.0, 0.0).astype(BF)
                pieces = jnp.concatenate([recv[hf, g, p] for g in range(8)], axis=0)
                sums = dot(pick, pieces, 1, 0).astype(BF)
                for l in range(OWN):
                    mid[hf, p, l] = sums[l * RH:(l + 1) * RH]
                return carry
            lax.fori_loop(0, 4, place, 0)
            for k in (1, 3, 2):
                line_msg(e, hf, k).start()
            part[hf, along[hf]] = mid[hf, along[hf]]

    def total(e, part, acc):
        line_arrived(e)
        for hf in (0, 1):
            rows = slice(hf * RH, (hf + 1) * RH)
            for l in range(OWN):
                acc[l, rows, :] = sum(part[hf, p, l].astype(F32) for p in range(4))

    def down_grads():
        scale_all(0)

        def go(j, carry):
            turned = jnp.transpose(scaled[0, j].astype(F32)).astype(BF)
            for k in (0, 1):
                b = 2 * j + k
                piece = dot(turned[k * R:(k + 1) * R], tok_of(b), 1, 0).astype(BF)
                for hf in (0, 1):
                    grads[hf, b] = piece[hf * RH:(hf + 1) * RH]
            return carry

        lax.fori_loop(0, NZ, go, 0)

    def up_grads():
        scale_all(1)

        def go(j, carry):
            mine = scaled[1, j]
            turned = jnp.transpose(mine.astype(F32)).astype(BF)
            for k in (0, 1):
                b = 2 * j + k
                piece = dot(turned[k * R:(k + 1) * R], cot_of(b), 1, 0).astype(BF)
                for hf in (0, 1):
                    hgrads[hf, b] = piece[hf * RH:(hf + 1) * RH]
            return carry

        lax.fori_loop(0, NZ, go, 0)

    def apart(mine):
        zero = jnp.zeros((), BF)
        return jnp.concatenate([jnp.where(lanes < R, mine, zero), jnp.where(lanes >= R, mine, zero)], axis=0)

    def lora_values():
        def go(j, carry):
            ups = of_blocks(urecv, 2 * j, 2 * j + 1)
            lorav[rows_of(j, CH), :] = dot(apart(scaled[1, j]), ups, 1, 0).astype(BF)
            return carry

        lax.fori_loop(0, NZ, go, 0)

    def base_chunk(cc):
        rows = rows_of(cc, CH)
        part = dot(tok[rows, :], w[...], 1, 0)
        for k in range(NZ):
            base[k, rows, :] = part[:, k * HEAD:(k + 1) * HEAD].astype(BF)

    def tig_chunk(cc):
        rows = rows_of(cc, CH)
        full = jnp.concatenate([cotf[k, rows, :] for k in range(NZ)], axis=1)
        part = dot(full, w[...], 1, 1)
        lora = dot(apart(scaled[0, cc]), of_blocks(drecv, 2 * cc, 2 * cc + 1), 1, 0).astype(BF).astype(F32)
        tigv[rows, :] = (part + lora).astype(BF)

    def rs(n, h, cc, dirn):
        rows = rows_of(cc, CH)
        if dirn == 0:
            dest, to = (z + h) % NZ, right
        else:
            dest, to = (z - h + NZ) % NZ, left
        return pltpu.make_async_remote_copy(
            src_ref=base.at[dest, rows], dst_ref=rsr.at[dirn, n], send_sem=rs_s.at[dirn, n],
            recv_sem=rs_r.at[dirn, n], device_id=(d, to), device_id_type=MESH)

    def rs_add(n_in, h, cc, dirn):
        rs(n_in, h, cc, dirn).wait_recv()
        dest = (z + h) % NZ if dirn == 0 else (z - h + NZ) % NZ
        rows = rows_of(cc, CH)
        base[dest, rows, :] = (base[dest, rows, :].astype(F32) + rsr[dirn, n_in].astype(F32)).astype(BF)

    def ag_step(m):
        for dirn in (0, 1):
            lag = NC - (m // (3 * NC)) * (NC // 2) * dirn

            @pl.when(m >= NC)
            def _():
                ag(m - lag, dirn).wait_recv()
            ag(m - DEPTH, dirn).wait_send()
            ag(m, dirn).start()

    def rs_step(n):
        @pl.when(n < DEPTH)
        def _():
            for dirn in (0, 1):
                ag(MSG - DEPTH + n, dirn).wait_send()

        @pl.when(n >= DEPTH)
        def _():
            for dirn in (0, 1):
                rs(n - DEPTH, 3, 0, dirn).wait_send()

        @pl.when(n < 4)
        def _():
            for dirn in (0, 1):
                rs(n, 4, n + dirn * 4, dirn).start()

        @pl.when(n >= 4)
        def _():
            k, cc = (n - 4) // NC, (n - 4) % NC
            for dirn in (0, 1):
                @pl.when((k == 0) & (cc // 4 == dirn))
                def _():
                    rs_add(cc - 4 * dirn, 3, cc, dirn)

                @pl.when(k > 0)
                def _():
                    rs_add(n - NC, 3 - k, cc, dirn)
                rs(n, 3 - k, cc, dirn).start()

    def ag_rest(m, carry):
        ag(m, 0).wait_recv()
        ag(m - NC // 2 + (m // (3 * NC)) * (NC // 2), 1).wait_recv()
        return carry

    def every(u, first, step, n, what):
        @pl.when((u >= first) & (u < first + n * step) & ((u - first) % step == 0))
        def _():
            what((u - first) // step)

    def hops(u, first, q, lo, hi):
        for k in range(9):
            if lo <= first + k * HOPS[q] < hi:
                @pl.when(u == first + k * HOPS[q])
                def _():
                    ar_step(q, k)

    def run(lo, hi, step):
        def at_slot(first, what, *args):
            if lo <= first < hi:
                @pl.when(u_now[0] == first)
                def _():
                    what(*args)

        u_now = [None]

        def slot(u, carry):
            u_now[0] = u
            step(u)
            at_slot(U_BACK, row_arrived, UP)
            at_slot(U_BACK, low_rank, 0, urecv, cot_of, 0, NZ)
            at_slot(U_HAND, hand_on, DOWN, dmid, dsend, drecv)
            at_slot(U_LOW, row_arrived, DOWN)
            at_slot(U_LOW, low_rank, 1, drecv, tok_of, 0, NZ // 2)
            at_slot(U_LOW + 1, low_rank, 1, drecv, tok_of, NZ // 2, NZ)
            hops(u, U_BACK_HOP, 0, lo, hi)
            hops(u, U_LOW_HOP, 1, lo, hi)
            if lo < U_BASE + 2 * NC and U_BASE < hi:
                every(u, U_BASE, 2, NC, base_chunk)
            at_slot(U_BACK_END, down_grads)
            at_slot(U_BACK_END + 1, send_grads, GRAD, grads, gsend, grecv)
            at_slot(U_TIG, lax.fori_loop, MSG - NC, MSG, ag_rest, 0)
            if lo < U_TIG + 2 * NC and U_TIG < hi:
                every(u, U_TIG, 2, NC, tig_chunk)
            at_slot(U_TALLY, row_arrived, GRAD)
            at_slot(U_TALLY, tally, GRAD, grecv, gmid, gpart, (0,))
            at_slot(U_TALLY + 1, tally, GRAD, grecv, gmid, gpart, (1,))
            at_slot(U_LOW_END, up_grads)
            at_slot(U_LOW_END + 1, send_grads, HGRAD, hgrads, hsend, hrecv)
            at_slot(U_LOW_END + 2, lora_values)
            at_slot(U_HTALLY, row_arrived, HGRAD)
            at_slot(U_HTALLY, tally, HGRAD, hrecv, hmid, hpart)
            return carry

        lax.fori_loop(lo, hi, slot, 0)

    run(DEPTH, MSG, ag_step)
    run(MSG, 2 * MSG, lambda u: rs_step(u - MSG))

    def finish(cc, carry):
        n = MSG - NC + cc
        rows = rows_of(cc, CH)
        for dirn in (0, 1):
            rs(n, 1, cc, dirn).wait_recv()
        whole = base[z, rows, :].astype(F32) + rsr[0, n].astype(F32) + rsr[1, n].astype(F32)
        valv[rows, :] = (whole + lorav[rows, :].astype(F32)).astype(BF)
        return carry

    total(GRAD, gpart, dacc)
    lax.fori_loop(0, NC, finish, 0)
    total(HGRAD, hpart, uacc)

    def rs_rest(n, carry):
        for dirn in (0, 1):
            rs(n, 3, 0, dirn).wait_send()
        return carry

    lax.fori_loop(MSG - DEPTH, MSG, rs_rest, 0)
    for e in (TAG, UP, DOWN, GRAD, HGRAD):
        each_row(e, lambda copy, hf, k2: copy.wait_send())
        if e != TAG:
            each_line(e, lambda copy: copy.wait_send())
    for q in (0, 1):
        for k in range(8):
            for dirn in (0, 1):
                ar_msg(q, k, dirn).wait_send()


def hand_out(*refs):
    n = len(refs) // 2
    copies = [pltpu.make_async_copy(refs[i], refs[n + i], refs[-1].at[i]) for i in range(n)]
    for copy in copies:
        copy.start()
    for copy in copies:
        copy.wait()


def on_device(tokens, cotangent, base_weight, adapter_down, adapter_up, block_adapter, adapter_slot, adapter_rank):
    vm, dma = pltpu.VMEM, pltpu.SemaphoreType.DMA
    smem = pl.BlockSpec(memory_space=pltpu.SMEM)
    vmem = pl.BlockSpec(memory_space=pltpu.VMEM)
    hbm = pl.BlockSpec(memory_space=pl.ANY)
    rh = R // 2
    scratch = [
        vm((ROWS, FEAT), BF), vm((NZ, ROWS, HEAD), BF), vm((FEAT, NZ * HEAD), BF),
        vm((OWN, R, FEAT), F32), vm((OWN, R, HEAD), F32), vm((2, OWN, rh, FEAT), BF), vm((2, OWN, rh, HEAD), BF),
        vm((NZ, ROWS, HEAD), BF), vm((2, MSG, CH, HEAD), BF),
        vm((8, 128), I32), vm((2, 8, 8, 128), I32), vm((2, 8, 128), I32), vm((8, 128), I32), vm((8, 128), F32),
        vm((2, 4, OWN, rh, HEAD), BF), vm((2, 8, 4, rh, HEAD), BF), vm((2, DP, rh, HEAD), BF),
        vm((2, 4, OWN, rh, FEAT), BF), vm((2, 8, 4, rh, FEAT), BF), vm((2, DP, rh, FEAT), BF),
        vm((2, NB, rh, FEAT), BF), vm((2, 8, 4, rh, FEAT), BF), vm((2, 8, 4, rh, FEAT), BF),
        vm((2, 4, OWN, rh, FEAT), BF), vm((2, 4, OWN, rh, FEAT), BF),
        vm((2, NB, rh, HEAD), BF), vm((2, 8, 4, rh, HEAD), BF), vm((2, 8, 4, rh, HEAD), BF),
        vm((2, 4, OWN, rh, HEAD), BF), vm((2, 4, OWN, rh, HEAD), BF),
        vm((2, NZ, BLK, 2 * R), BF), vm((2, 2, 4, BLK, 2 * R), BF), vm((2, NZ, BLK, 2 * R), BF), vm((2, NZ, BLK, 2 * R), BF),
        vm((ROWS, HEAD), BF),
        pltpu.SMEM((2, 8, 128), I32), pltpu.SMEM((8, 128), I32),
        dma((5,)),
        dma((2, MSG)), dma((2, MSG)), dma((2, MSG)), dma((2, MSG)),
        dma((2, 2, 8)), dma((2, 2, 8)),
        dma((5, 2, 8)), dma((5, 2, 8)), dma((5, 2, 4)), dma((5, 2, 4)), dma((2,)),
    ]
    val, tig, dmg, umg = pl.pallas_call(
        kernel,
        out_shape=(
            vm((ROWS, HEAD), BF), vm((ROWS, FEAT), BF), vm((OWN, R, FEAT), F32), vm((OWN, R, HEAD), F32)),
        in_specs=[smem, smem, smem, vmem, vmem, hbm, hbm, hbm, hbm, hbm],
        out_specs=(vmem,) * 4,
        scratch_shapes=scratch,
        compiler_params=pltpu.CompilerParams(
            collective_id=0, has_side_effects=True, vmem_limit_bytes=54 * 2**20),
    )(
        block_adapter, adapter_slot, adapter_rank,
        adapter_slot.reshape(1, -1), adapter_rank.reshape(1, -1),
        tokens, cotangent, base_weight, jnp.swapaxes(adapter_down, 1, 2), adapter_up,
    )
    outs = (val, tig, dmg, umg)
    val, tig, dmg, umg = pl.pallas_call(
        hand_out,
        out_shape=tuple(jax.ShapeDtypeStruct(o.shape, o.dtype) for o in outs),
        in_specs=[vmem] * 4,
        out_specs=(hbm,) * 4,
        scratch_shapes=[dma((4,))],
        compiler_params=pltpu.CompilerParams(vmem_limit_bytes=4 * 2**20),
    )(*outs)
    return val, tig, jnp.swapaxes(dmg, 1, 2), umg


def solution(mesh):
    return jax.shard_map(
        on_device,
        mesh=mesh,
        in_specs=(
            P("dp", "tensor"), P("dp", "tensor"), P("tensor", None), P("dp", "tensor", None),
            P("dp", None, "tensor"), P("dp"), P(), P(),
        ),
        out_specs=(P("dp", "tensor"), P("dp", "tensor"), P("dp", "tensor", None), P("dp", None, "tensor")),
        check_vma=False,
    )
```

```python
import functools

import jax
import jax.numpy as jnp
from jax import lax
from jax.experimental import pallas as pl
from jax.experimental.pallas import tpu as pltpu
from jax.sharding import PartitionSpec as P

MESH = pl.DeviceIdType.MESH
BF, F32, I32 = jnp.bfloat16, jnp.float32, jnp.int32
DP, NZ = 32, 8
ROWS, FEAT, HEAD, R, BLK, NB, OWN = 2048, 640, 128, 64, 128, 16, 4
CH = 256
NC = ROWS // CH
MSG = 3 * NC + NC // 2
DEPTH = 3
U_BACK = 8
U_HAND = 11
U_LOW = 24
HOPS = (3, 3)
U_BACK_HOP = U_BACK + 1
U_LOW_HOP = U_LOW + 2
U_BACK_END = U_BACK_HOP + 8 * HOPS[0]
U_LOW_END = U_LOW_HOP + 8 * HOPS[1]
U_BASE = 9
U_TIG = U_BACK_END + 2
U_TALLY = 46
U_HTALLY = U_LOW_END + 4
U_SENT = 30


def dot(a, b, ca, cb):
    return lax.dot_general(a, b, (((ca,), (cb,)), ((), ())), preferred_element_type=F32)


def kernel(
    ba_s, slot_s, rank_s, slot_v, rank_v, tok_h, cot_h, w_h, dn_h, up_h,
    valv, tigv, dacc, uacc,
    tok, cotf, w, dnf, upf, dnb, upb, base, rsr, reqs, tagr, tag_v, bi_v, scale,
    umid, usend, urecv, dmid, dsend, drecv, grads, gsend, grecv, gmid, gpart, hgrads, hsend, hrecv, hmid, hpart,
    arp, arr, tot, scaled, lorav, tag_s, bi_s,
    in_sem, ag_s, ag_r, rs_s, rs_r, ar_s, ar_r, row_s, row_r, line_s, line_r, sm_sem,
):
    d = lax.axis_index("dp")
    z = lax.axis_index("tensor")
    x, y, c = d // 8, (d // 2) % 4, d % 2
    right, left = (z + 1) % NZ, (z + NZ - 1) % NZ

    cp_cot = pltpu.make_async_copy(cot_h, cotf.at[z], in_sem.at[0])
    cp_up = pltpu.make_async_copy(up_h, upf, in_sem.at[1])
    cp_dn = pltpu.make_async_copy(dn_h, dnf, in_sem.at[2])
    cp_tok = pltpu.make_async_copy(tok_h, tok, in_sem.at[3])
    cp_w = pltpu.make_async_copy(w_h, w, in_sem.at[4])
    for cp in (cp_cot, cp_up, cp_dn, cp_tok, cp_w):
        cp.start()

    barrier = pltpu.get_barrier_semaphore()

    def at(px, py, pc):
        return px * 8 + py * 2 + pc

    def beyond(hf, k2):
        ahead, core = k2 // 2, (c + k2 % 2) % 2
        if hf == 0:
            pos = (x + ahead) % 4
            return pos * 2 + core, at(pos, y, core)
        pos = (y + ahead) % 4
        return pos * 2 + core, at(x, pos, core)

    def greet(k2, carry):
        for hf in (0, 1):
            pl.semaphore_signal(barrier, inc=1, device_id=(beyond(hf, k2)[1], z), device_id_type=MESH)
        return carry

    for to in (right, left):
        pl.semaphore_signal(barrier, inc=1, device_id=(d, to), device_id_type=MESH)
    lax.fori_loop(1, 8, greet, 0)

    pair2 = lax.broadcasted_iota(I32, (8, 128), 0)
    lane2 = lax.broadcasted_iota(I32, (8, 128), 1)
    tags = jnp.zeros((8, 128), I32)
    which = jnp.zeros((8, 128), I32)
    ranks = jnp.ones((8, 128), I32)
    for b in range(NB):
        a = ba_s[b]
        s = slot_s[a]
        o = s // OWN
        tags = jnp.where(lane2 == o, s - o * OWN + 1, tags)
        which = jnp.where(lane2 == o, b, which)
        here = (pair2 == b // 2) & ((lane2 >= R) if b % 2 else (lane2 < R))
        ranks = jnp.where(here, rank_s[a], ranks)
    reqs[...] = tags
    bi_v[...] = which
    scale[...] = R / (4.0 * ranks.astype(F32))
    cp_bi = pltpu.make_async_copy(bi_v, bi_s, sm_sem.at[0])
    cp_bi.start()
    pl.semaphore_wait(barrier, 16)

    def ag(m, dirn):
        h, cc = m // NC, m % NC
        row = cc * CH
        if dirn == 0:
            shard, to = (z - h + NZ) % NZ, right
        else:
            shard, to = (z + h) % NZ, left
            row = row + (h // 3) * (ROWS // 2)
        part = cotf.at[shard, pl.ds(pl.multiple_of(row, CH), CH)]
        return pltpu.make_async_remote_copy(
            src_ref=part, dst_ref=part, send_sem=ag_s.at[dirn, m], recv_sem=ag_r.at[dirn, m],
            device_id=(d, to), device_id_type=MESH)

    cp_cot.wait()

    def ag_first(m, carry):
        ag(m, 0).start()
        ag(m, 1).start()
        return carry

    lax.fori_loop(0, DEPTH, ag_first, 0)

    along = (y, x)
    across = (x, y)
    me8 = tuple(q * 2 + c for q in across)

    def owner(hf, p, q, core):
        return at(q, p, core) if hf == 0 else at(p, q, core)

    def row_copy(e, hf, k2, src, dst):
        return pltpu.make_async_remote_copy(
            src_ref=src, dst_ref=dst, send_sem=row_s.at[e, hf, k2], recv_sem=row_r.at[e, hf, k2],
            device_id=(beyond(hf, k2)[1], z), device_id_type=MESH)

    def line_copy(e, hf, k, src, dst):
        to = at(x, (y + k) % 4, c) if hf == 0 else at((x + k) % 4, y, c)
        return pltpu.make_async_remote_copy(
            src_ref=src, dst_ref=dst, send_sem=line_s.at[e, hf, k], recv_sem=line_r.at[e, hf, k],
            device_id=(to, z), device_id_type=MESH)

    TAG, UP, DOWN, GRAD, HGRAD = 0, 1, 2, 3, 4

    def row_msg(e, hf, k2):
        if e == TAG:
            return row_copy(e, hf, k2, reqs, tagr.at[hf, me8[hf]])
        g = beyond(hf, k2)[0]
        if e in (UP, DOWN):
            src, dst = ((usend, urecv), (dsend, drecv))[e - UP]
            return row_copy(e, hf, k2, src.at[hf, g], dst.at[hf, pl.ds(me8[hf] * 4, 4)])
        src, dst = ((gsend, grecv), (hsend, hrecv))[e - GRAD]
        return row_copy(e, hf, k2, src.at[hf, g], dst.at[hf, me8[hf]])

    def line_msg(e, hf, k):
        p = along[hf]
        if e in (UP, DOWN):
            src, dst = ((upb, umid), (dnb, dmid))[e - UP]
            return line_copy(e, hf, k, src.at[hf], dst.at[hf, p])
        src, dst = ((gmid, gpart), (hmid, hpart))[e - GRAD]
        return line_copy(e, hf, k, src.at[hf, (p + k) % 4], dst.at[hf, p])

    def each_row(e, what):
        def go(j, carry):
            k2 = (j * 3) % 8
            for hf in (0, 1):
                what(row_msg(e, hf, k2), hf, k2)
            return carry
        lax.fori_loop(1, 8, go, 0)

    def each_line(e, what):
        for k in (1, 3, 2):
            for hf in (0, 1):
                what(line_msg(e, hf, k))

    def row_arrived(e):
        each_row(e, lambda copy, hf, k2: copy.wait_recv())

    def line_arrived(e):
        each_line(e, lambda copy: copy.wait_recv())

    def row_sent(e):
        each_row(e, lambda copy, hf, k2: copy.wait_send())

    def line_sent(e):
        each_line(e, lambda copy: copy.wait_send())

    each_row(TAG, lambda copy, hf, k2: copy.start())
    for hf in (0, 1):
        tagr[hf, me8[hf]] = reqs[...]

    cp_up.wait()
    cp_dn.wait()
    RH = R // 2
    for l in range(OWN):
        mine = slot_v[...] == d * OWN + l
        rank = jnp.sum(jnp.where(mine, rank_v[...], 0), axis=1, keepdims=True)
        for hf in (0, 1):
            rows = slice(hf * RH, (hf + 1) * RH)
            keep = lax.broadcasted_iota(I32, (RH, HEAD), 0) + hf * RH < rank
            upb[hf, l] = jnp.where(keep, upf[l, rows, :], 0.0).astype(BF)
    each_line(UP, lambda copy: copy.start())
    for l in range(OWN):
        mine = slot_v[...] == d * OWN + l
        rank = jnp.sum(jnp.where(mine, rank_v[...], 0), axis=1, keepdims=True)
        for hf in (0, 1):
            rows = slice(hf * RH, (hf + 1) * RH)
            keep = lax.broadcasted_iota(I32, (RH, FEAT), 0) + hf * RH < rank
            dnb[hf, l] = jnp.where(keep, dnf[l, rows, :], 0.0).astype(BF)
    for hf in (0, 1):
        umid[hf, along[hf]] = upb[hf]
        dmid[hf, along[hf]] = dnb[hf]
    row_arrived(TAG)
    for hf in (0, 1):
        tag_v[hf] = tagr[hf, :, 0, :]
    cp_tag = pltpu.make_async_copy(tag_v, tag_s, sm_sem.at[1])
    cp_tag.start()
    cp_tag.wait()

    def wanted(hf, g, p):
        return tag_s[hf, g, owner(hf, p, across[hf], c)]

    def hand_on(e, mid, send, recv):
        line_arrived(e)

        def go(copy, hf, k2):
            g = beyond(hf, k2)[0]
            for p in range(4):
                send[hf, g, p] = mid[hf, p, jnp.maximum(wanted(hf, g, p) - 1, 0)]
            copy.start()

        each_row(e, go)
        for hf in (0, 1):
            for p in range(4):
                recv[hf, me8[hf] * 4 + p] = mid[hf, p, jnp.maximum(wanted(hf, me8[hf], p) - 1, 0)]

    hand_on(UP, umid, usend, urecv)
    each_line(DOWN, lambda copy: copy.start())
    cp_bi.wait()
    cp_tok.wait()
    cp_w.wait()

    def of_block(recv, b):
        o = slot_s[ba_s[b]] // OWN
        ox, oy, oc = o // 8, (o // 2) % 4, o % 2
        return [recv[0, (ox * 2 + oc) * 4 + oy], recv[1, (oy * 2 + oc) * 4 + ox]]

    def of_blocks(recv, *bs):
        return jnp.concatenate([part for b in bs for part in of_block(recv, b)], axis=0)

    half = (slice(0, BLK // 2), slice(BLK // 2, BLK))

    def ar_copy(q, k, dirn, src, dst):
        return pltpu.make_async_remote_copy(
            src_ref=src, dst_ref=dst, send_sem=ar_s.at[q, dirn, k], recv_sem=ar_r.at[q, dirn, k],
            device_id=(d, (right, left)[dirn]), device_id_type=MESH)

    def ar_msg(q, k, dirn):
        sgn = (1, -1)[dirn]
        if k == 0:
            p = (z + 4) % NZ
            lo = (0, BLK // 2)[dirn]
            return ar_copy(q, k, dirn, arp.at[q, p, pl.ds(lo, BLK // 2)], arr.at[q, dirn, 0, pl.ds(lo, BLK // 2)])
        if k < 4:
            p = (z + sgn * (4 - k) + NZ) % NZ
            return ar_copy(q, k, dirn, arp.at[q, p], arr.at[q, dirn, k])
        p = (z - sgn * (k - 4) + NZ) % NZ
        if k < 7:
            return ar_copy(q, k, dirn, tot.at[q, p], tot.at[q, p])
        lo = (0, BLK // 2)[dirn]
        part = tot.at[q, p, pl.ds(lo, BLK // 2)]
        return ar_copy(q, k, dirn, part, part)

    def ar_step(q, k):
        if k > 0:
            for dirn in (0, 1):
                ar_msg(q, k - 1, dirn).wait_recv()
        if k in (1, 2, 3):
            for dirn in (0, 1):
                p = (z + (1, -1)[dirn] * (4 - k) + NZ) % NZ
                rows = half[dirn] if k == 1 else slice(0, BLK)
                arp[q, p, rows] = (arp[q, p, rows].astype(F32) + arr[q, dirn, k - 1, rows].astype(F32)).astype(BF)
        if k == 4:
            tot[q, z] = (arp[q, z].astype(F32) + arr[q, 0, 3].astype(F32) + arr[q, 1, 3].astype(F32)).astype(BF)
        if k < 8:
            for dirn in (0, 1):
                ar_msg(q, k, dirn).start()

    def ar_sent(q):
        for k in range(8):
            for dirn in (0, 1):
                ar_msg(q, k, dirn).wait_send()

    def scale_all(q):
        def go(j, carry):
            scaled[q, j] = (scale[pl.ds(j, 1), :] * tot[q, j].astype(F32)).astype(BF)
            return carry
        lax.fori_loop(0, NZ, go, 0)

    lanes = lax.broadcasted_iota(I32, (BLK, 2 * R), 1)

    def rows_of(b, n=BLK):
        return pl.ds(pl.multiple_of(b * n, n), n)

    def low_rank(q, recv, data, lo, hi):
        def go(j, carry):
            parts = [dot(data(2 * j + k), of_blocks(recv, 2 * j + k), 1, 1) for k in (0, 1)]
            arp[q, j] = jnp.concatenate(parts, axis=1).astype(BF)
            return carry

        lax.fori_loop(lo, hi, go, 0)

    def tok_of(b):
        return tok[rows_of(b), :]

    def cot_of(b):
        return cotf[z, rows_of(b), :]

    def send_grads(e, src, send, recv):
        def pick(hf, q, core, p):
            return src[hf, bi_s[0, owner(hf, p, q, core)]]

        def go(copy, hf, k2):
            g = beyond(hf, k2)[0]
            for p in range(4):
                send[hf, g, p] = pick(hf, g // 2, g % 2, p)
            copy.start()

        each_row(e, go)
        for hf in (0, 1):
            for p in range(4):
                recv[hf, me8[hf], p] = pick(hf, across[hf], c, p)

    def tally(e, recv, mid, part, halves=(0, 1)):
        shape = (OWN * RH, 8 * RH)
        to, frm = lax.broadcasted_iota(I32, shape, 0), lax.broadcasted_iota(I32, shape, 1)
        same_row = (to % RH) == (frm % RH)
        slot, core = to // RH + 1, frm // RH
        for hf in halves:
            def place(p, carry):
                tags = jnp.zeros(shape, I32)
                for g in range(8):
                    tags = jnp.where(core == g, wanted(hf, g, p), tags)
                pick = jnp.where(same_row & (tags == slot), 1.0, 0.0).astype(BF)
                pieces = jnp.concatenate([recv[hf, g, p] for g in range(8)], axis=0)
                sums = dot(pick, pieces, 1, 0).astype(BF)
                for l in range(OWN):
                    mid[hf, p, l] = sums[l * RH:(l + 1) * RH]
                return carry
            lax.fori_loop(0, 4, place, 0)
            for k in (1, 3, 2):
                line_msg(e, hf, k).start()
            part[hf, along[hf]] = mid[hf, along[hf]]

    def total(e, part, acc):
        line_arrived(e)
        for hf in (0, 1):
            rows = slice(hf * RH, (hf + 1) * RH)
            for l in range(OWN):
                acc[l, rows, :] = sum(part[hf, p, l].astype(F32) for p in range(4))

    def down_grads():
        scale_all(0)

        def go(j, carry):
            turned = jnp.transpose(scaled[0, j].astype(F32)).astype(BF)
            for k in (0, 1):
                b = 2 * j + k
                piece = dot(turned[k * R:(k + 1) * R], tok_of(b), 1, 0).astype(BF)
                for hf in (0, 1):
                    grads[hf, b] = piece[hf * RH:(hf + 1) * RH]
            return carry

        lax.fori_loop(0, NZ, go, 0)

    def up_grads():
        scale_all(1)

        def go(j, carry):
            mine = scaled[1, j]
            turned = jnp.transpose(mine.astype(F32)).astype(BF)
            for k in (0, 1):
                b = 2 * j + k
                piece = dot(turned[k * R:(k + 1) * R], cot_of(b), 1, 0).astype(BF)
                for hf in (0, 1):
                    hgrads[hf, b] = piece[hf * RH:(hf + 1) * RH]
            return carry

        lax.fori_loop(0, NZ, go, 0)

    def apart(mine):
        zero = jnp.zeros((), BF)
        return jnp.concatenate([jnp.where(lanes < R, mine, zero), jnp.where(lanes >= R, mine, zero)], axis=0)

    def lora_values():
        def go(j, carry):
            ups = of_blocks(urecv, 2 * j, 2 * j + 1)
            lorav[rows_of(j, CH), :] = dot(apart(scaled[1, j]), ups, 1, 0).astype(BF)
            return carry

        lax.fori_loop(0, NZ, go, 0)

    def base_chunk(cc):
        rows = rows_of(cc, CH)
        part = dot(tok[rows, :], w[...], 1, 0)
        for k in range(NZ):
            base[k, rows, :] = part[:, k * HEAD:(k + 1) * HEAD].astype(BF)

    def tig_chunk(cc):
        rows = rows_of(cc, CH)
        full = jnp.concatenate([cotf[k, rows, :] for k in range(NZ)], axis=1)
        part = dot(full, w[...], 1, 1)
        lora = dot(apart(scaled[0, cc]), of_blocks(drecv, 2 * cc, 2 * cc + 1), 1, 0).astype(BF).astype(F32)
        tigv[rows, :] = (part + lora).astype(BF)

    def rs(n, h, cc, dirn):
        rows = rows_of(cc, CH)
        if dirn == 0:
            dest, to = (z + h) % NZ, right
        else:
            dest, to = (z - h + NZ) % NZ, left
        return pltpu.make_async_remote_copy(
            src_ref=base.at[dest, rows], dst_ref=rsr.at[dirn, n], send_sem=rs_s.at[dirn, n],
            recv_sem=rs_r.at[dirn, n], device_id=(d, to), device_id_type=MESH)

    def rs_add(n_in, h, cc, dirn):
        rs(n_in, h, cc, dirn).wait_recv()
        dest = (z + h) % NZ if dirn == 0 else (z - h + NZ) % NZ
        rows = rows_of(cc, CH)
        base[dest, rows, :] = (base[dest, rows, :].astype(F32) + rsr[dirn, n_in].astype(F32)).astype(BF)

    def ag_step(m):
        for dirn in (0, 1):
            lag = NC - (m // (3 * NC)) * (NC // 2) * dirn

            @pl.when(m >= NC)
            def _():
                ag(m - lag, dirn).wait_recv()
            ag(m - DEPTH, dirn).wait_send()
            ag(m, dirn).start()

    def rs_step(n):
        @pl.when(n < DEPTH)
        def _():
            for dirn in (0, 1):
                ag(MSG - DEPTH + n, dirn).wait_send()

        @pl.when(n >= DEPTH)
        def _():
            for dirn in (0, 1):
                rs(n - DEPTH, 3, 0, dirn).wait_send()

        @pl.when(n < 4)
        def _():
            for dirn in (0, 1):
                rs(n, 4, n + dirn * 4, dirn).start()

        @pl.when(n >= 4)
        def _():
            k, cc = (n - 4) // NC, (n - 4) % NC
            for dirn in (0, 1):
                @pl.when((k == 0) & (cc // 4 == dirn))
                def _():
                    rs_add(cc - 4 * dirn, 3, cc, dirn)

                @pl.when(k > 0)
                def _():
                    rs_add(n - NC, 3 - k, cc, dirn)
                rs(n, 3 - k, cc, dirn).start()

    def ag_rest(m, carry):
        ag(m, 0).wait_recv()
        ag(m - NC // 2 + (m // (3 * NC)) * (NC // 2), 1).wait_recv()
        return carry

    def every(u, first, step, n, what):
        @pl.when((u >= first) & (u < first + n * step) & ((u - first) % step == 0))
        def _():
            what((u - first) // step)

    def hops(u, first, q, lo, hi):
        for k in range(9):
            if lo <= first + k * HOPS[q] < hi:
                @pl.when(u == first + k * HOPS[q])
                def _():
                    ar_step(q, k)

    def run(lo, hi, step):
        def at_slot(first, what, *args):
            if lo <= first < hi:
                @pl.when(u_now[0] == first)
                def _():
                    what(*args)

        u_now = [None]

        def slot(u, carry):
            u_now[0] = u
            step(u)
            at_slot(U_BACK, row_arrived, UP)
            at_slot(U_BACK, low_rank, 0, urecv, cot_of, 0, NZ)
            at_slot(U_HAND, hand_on, DOWN, dmid, dsend, drecv)
            at_slot(U_LOW, row_arrived, DOWN)
            at_slot(U_LOW, low_rank, 1, drecv, tok_of, 0, NZ // 2)
            at_slot(U_LOW + 1, low_rank, 1, drecv, tok_of, NZ // 2, NZ)
            hops(u, U_BACK_HOP, 0, lo, hi)
            hops(u, U_LOW_HOP, 1, lo, hi)
            if lo < U_BASE + 2 * NC and U_BASE < hi:
                every(u, U_BASE, 2, NC, base_chunk)
            at_slot(U_BACK_END, down_grads)
            at_slot(U_BACK_END + 1, send_grads, GRAD, grads, gsend, grecv)
            at_slot(U_TIG, lax.fori_loop, MSG - NC, MSG, ag_rest, 0)
            if lo < U_TIG + 2 * NC and U_TIG < hi:
                every(u, U_TIG, 2, NC, tig_chunk)
            at_slot(U_TALLY, row_arrived, GRAD)
            at_slot(U_TALLY, tally, GRAD, grecv, gmid, gpart, (0,))
            at_slot(U_TALLY + 1, tally, GRAD, grecv, gmid, gpart, (1,))
            at_slot(U_LOW_END, up_grads)
            at_slot(U_LOW_END + 1, send_grads, HGRAD, hgrads, hsend, hrecv)
            at_slot(U_LOW_END + 2, lora_values)
            at_slot(U_SENT, row_sent, TAG)
            at_slot(U_SENT, line_sent, UP)
            at_slot(U_SENT + 2, row_sent, UP)
            at_slot(U_SENT + 4, line_sent, DOWN)
            at_slot(U_SENT + 8, row_sent, DOWN)
            at_slot(U_SENT + 10, ar_sent, 0)
            at_slot(U_TALLY + 4, row_sent, GRAD)
            at_slot(U_LOW_END + 3, ar_sent, 1)
            at_slot(U_HTALLY, row_arrived, HGRAD)
            at_slot(U_HTALLY, tally, HGRAD, hrecv, hmid, hpart)
            return carry

        lax.fori_loop(lo, hi, slot, 0)

    run(DEPTH, MSG, ag_step)
    run(MSG, 2 * MSG, lambda u: rs_step(u - MSG))

    def finish(cc, carry):
        n = MSG - NC + cc
        rows = rows_of(cc, CH)
        for dirn in (0, 1):
            rs(n, 1, cc, dirn).wait_recv()
        whole = base[z, rows, :].astype(F32) + rsr[0, n].astype(F32) + rsr[1, n].astype(F32)
        valv[rows, :] = (whole + lorav[rows, :].astype(F32)).astype(BF)
        return carry

    total(GRAD, gpart, dacc)
    lax.fori_loop(0, NC, finish, 0)
    total(HGRAD, hpart, uacc)

    def rs_rest(n, carry):
        for dirn in (0, 1):
            rs(n, 3, 0, dirn).wait_send()
        return carry

    lax.fori_loop(MSG - DEPTH, MSG, rs_rest, 0)
    for e in (GRAD, HGRAD):
        line_sent(e)
    row_sent(HGRAD)


def hand_out(*refs):
    n = len(refs) // 2
    copies = [pltpu.make_async_copy(refs[i], refs[n + i], refs[-1].at[i]) for i in range(n)]
    for copy in copies:
        copy.start()
    for copy in copies:
        copy.wait()


def on_device(tokens, cotangent, base_weight, adapter_down, adapter_up, block_adapter, adapter_slot, adapter_rank):
    vm, dma = pltpu.VMEM, pltpu.SemaphoreType.DMA
    smem = pl.BlockSpec(memory_space=pltpu.SMEM)
    vmem = pl.BlockSpec(memory_space=pltpu.VMEM)
    hbm = pl.BlockSpec(memory_space=pl.ANY)
    rh = R // 2
    scratch = [
        vm((ROWS, FEAT), BF), vm((NZ, ROWS, HEAD), BF), vm((FEAT, NZ * HEAD), BF),
        vm((OWN, R, FEAT), F32), vm((OWN, R, HEAD), F32), vm((2, OWN, rh, FEAT), BF), vm((2, OWN, rh, HEAD), BF),
        vm((NZ, ROWS, HEAD), BF), vm((2, MSG, CH, HEAD), BF),
        vm((8, 128), I32), vm((2, 8, 8, 128), I32), vm((2, 8, 128), I32), vm((8, 128), I32), vm((8, 128), F32),
        vm((2, 4, OWN, rh, HEAD), BF), vm((2, 8, 4, rh, HEAD), BF), vm((2, DP, rh, HEAD), BF),
        vm((2, 4, OWN, rh, FEAT), BF), vm((2, 8, 4, rh, FEAT), BF), vm((2, DP, rh, FEAT), BF),
        vm((2, NB, rh, FEAT), BF), vm((2, 8, 4, rh, FEAT), BF), vm((2, 8, 4, rh, FEAT), BF),
        vm((2, 4, OWN, rh, FEAT), BF), vm((2, 4, OWN, rh, FEAT), BF),
        vm((2, NB, rh, HEAD), BF), vm((2, 8, 4, rh, HEAD), BF), vm((2, 8, 4, rh, HEAD), BF),
        vm((2, 4, OWN, rh, HEAD), BF), vm((2, 4, OWN, rh, HEAD), BF),
        vm((2, NZ, BLK, 2 * R), BF), vm((2, 2, 4, BLK, 2 * R), BF), vm((2, NZ, BLK, 2 * R), BF), vm((2, NZ, BLK, 2 * R), BF),
        vm((ROWS, HEAD), BF),
        pltpu.SMEM((2, 8, 128), I32), pltpu.SMEM((8, 128), I32),
        dma((5,)),
        dma((2, MSG)), dma((2, MSG)), dma((2, MSG)), dma((2, MSG)),
        dma((2, 2, 8)), dma((2, 2, 8)),
        dma((5, 2, 8)), dma((5, 2, 8)), dma((5, 2, 4)), dma((5, 2, 4)), dma((2,)),
    ]
    val, tig, dmg, umg = pl.pallas_call(
        kernel,
        out_shape=(
            vm((ROWS, HEAD), BF), vm((ROWS, FEAT), BF), vm((OWN, R, FEAT), F32), vm((OWN, R, HEAD), F32)),
        in_specs=[smem, smem, smem, vmem, vmem, hbm, hbm, hbm, hbm, hbm],
        out_specs=(vmem,) * 4,
        scratch_shapes=scratch,
        compiler_params=pltpu.CompilerParams(
            collective_id=0, has_side_effects=True, vmem_limit_bytes=54 * 2**20),
    )(
        block_adapter, adapter_slot, adapter_rank,
        adapter_slot.reshape(1, -1), adapter_rank.reshape(1, -1),
        tokens, cotangent, base_weight, jnp.swapaxes(adapter_down, 1, 2), adapter_up,
    )
    outs = (val, tig, dmg, umg)
    val, tig, dmg, umg = pl.pallas_call(
        hand_out,
        out_shape=tuple(jax.ShapeDtypeStruct(o.shape, o.dtype) for o in outs),
        in_specs=[vmem] * 4,
        out_specs=(hbm,) * 4,
        scratch_shapes=[dma((4,))],
        compiler_params=pltpu.CompilerParams(vmem_limit_bytes=4 * 2**20),
    )(*outs)
    return val, tig, jnp.swapaxes(dmg, 1, 2), umg


def solution(mesh):
    return jax.shard_map(
        on_device,
        mesh=mesh,
        in_specs=(
            P("dp", "tensor"), P("dp", "tensor"), P("tensor", None), P("dp", "tensor", None),
            P("dp", None, "tensor"), P("dp"), P(), P(),
        ),
        out_specs=(P("dp", "tensor"), P("dp", "tensor"), P("dp", "tensor", None), P("dp", None, "tensor")),
        check_vma=False,
    )
```

```python
import functools

import jax
import jax.numpy as jnp
from jax import lax
from jax.experimental import pallas as pl
from jax.experimental.pallas import tpu as pltpu
from jax.sharding import PartitionSpec as P

MESH = pl.DeviceIdType.MESH
BF, F32, I32 = jnp.bfloat16, jnp.float32, jnp.int32
DP, NZ = 32, 8
ROWS, FEAT, HEAD, R, BLK, NB, OWN = 2048, 640, 128, 64, 128, 16, 4
CH = 256
NC = ROWS // CH
MSG = 3 * NC + NC // 2
DEPTH = 4
U_BACK = 8
U_HAND = 11
U_LOW = 24
HOPS = (3, 3)
U_BACK_HOP = U_BACK + 1
U_LOW_HOP = U_LOW + 2
U_BACK_END = U_BACK_HOP + 8 * HOPS[0]
U_LOW_END = U_LOW_HOP + 8 * HOPS[1]
U_BASE = 9
U_TIG = U_BACK_END + 2
U_TALLY = 46
U_HTALLY = U_LOW_END + 4
U_SENT = 30


def dot(a, b, ca, cb):
    return lax.dot_general(a, b, (((ca,), (cb,)), ((), ())), preferred_element_type=F32)


def kernel(
    ba_s, slot_s, rank_s, slot_v, rank_v, tok_h, cot_h, w_h, dn_h, up_h,
    valv, tigv, dacc, uacc,
    tok, cotf, w, dnf, upf, dnb, upb, base, rsr, reqs, tagr, tag_v, bi_v, scale,
    umid, usend, urecv, dmid, dsend, drecv, grads, gsend, grecv, gmid, gpart, hgrads, hsend, hrecv, hmid, hpart,
    arp, arr, tot, scaled, lorav, picks, tag_s, bi_s,
    in_sem, ag_s, ag_r, rs_s, rs_r, ar_s, ar_r, row_s, row_r, line_s, line_r, sm_sem,
):
    d = lax.axis_index("dp")
    z = lax.axis_index("tensor")
    x, y, c = d // 8, (d // 2) % 4, d % 2
    right, left = (z + 1) % NZ, (z + NZ - 1) % NZ

    cp_cot = pltpu.make_async_copy(cot_h, cotf.at[z], in_sem.at[0])
    cp_up = pltpu.make_async_copy(up_h, upf, in_sem.at[1])
    cp_dn = pltpu.make_async_copy(dn_h, dnf, in_sem.at[2])
    cp_tok = pltpu.make_async_copy(tok_h, tok, in_sem.at[3])
    cp_w = pltpu.make_async_copy(w_h, w, in_sem.at[4])
    for cp in (cp_cot, cp_up, cp_dn, cp_tok, cp_w):
        cp.start()

    barrier = pltpu.get_barrier_semaphore()

    def at(px, py, pc):
        return px * 8 + py * 2 + pc

    def beyond(hf, k2):
        ahead, core = k2 // 2, (c + k2 % 2) % 2
        if hf == 0:
            pos = (x + ahead) % 4
            return pos * 2 + core, at(pos, y, core)
        pos = (y + ahead) % 4
        return pos * 2 + core, at(x, pos, core)

    def greet(k2, carry):
        for hf in (0, 1):
            pl.semaphore_signal(barrier, inc=1, device_id=(beyond(hf, k2)[1], z), device_id_type=MESH)
        return carry

    for to in (right, left):
        pl.semaphore_signal(barrier, inc=1, device_id=(d, to), device_id_type=MESH)
    lax.fori_loop(1, 8, greet, 0)

    pair2 = lax.broadcasted_iota(I32, (8, 128), 0)
    lane2 = lax.broadcasted_iota(I32, (8, 128), 1)
    tags = jnp.zeros((8, 128), I32)
    which = jnp.zeros((8, 128), I32)
    ranks = jnp.ones((8, 128), I32)
    for b in range(NB):
        a = ba_s[b]
        s = slot_s[a]
        o = s // OWN
        tags = jnp.where(lane2 == o, s - o * OWN + 1, tags)
        which = jnp.where(lane2 == o, b, which)
        here = (pair2 == b // 2) & ((lane2 >= R) if b % 2 else (lane2 < R))
        ranks = jnp.where(here, rank_s[a], ranks)
    reqs[...] = tags
    bi_v[...] = which
    scale[...] = R / (4.0 * ranks.astype(F32))
    cp_bi = pltpu.make_async_copy(bi_v, bi_s, sm_sem.at[0])
    cp_bi.start()
    pl.semaphore_wait(barrier, 16)

    def ag(m, dirn):
        h, cc = m // NC, m % NC
        row = cc * CH
        if dirn == 0:
            shard, to = (z - h + NZ) % NZ, right
        else:
            shard, to = (z + h) % NZ, left
            row = row + (h // 3) * (ROWS // 2)
        part = cotf.at[shard, pl.ds(pl.multiple_of(row, CH), CH)]
        return pltpu.make_async_remote_copy(
            src_ref=part, dst_ref=part, send_sem=ag_s.at[dirn, m], recv_sem=ag_r.at[dirn, m],
            device_id=(d, to), device_id_type=MESH)

    cp_cot.wait()

    def ag_first(m, carry):
        ag(m, 0).start()
        ag(m, 1).start()
        return carry

    lax.fori_loop(0, DEPTH, ag_first, 0)

    along = (y, x)
    across = (x, y)
    me8 = tuple(q * 2 + c for q in across)

    def owner(hf, p, q, core):
        return at(q, p, core) if hf == 0 else at(p, q, core)

    def row_copy(e, hf, k2, src, dst):
        return pltpu.make_async_remote_copy(
            src_ref=src, dst_ref=dst, send_sem=row_s.at[e, hf, k2], recv_sem=row_r.at[e, hf, k2],
            device_id=(beyond(hf, k2)[1], z), device_id_type=MESH)

    def line_copy(e, hf, k, src, dst):
        to = at(x, (y + k) % 4, c) if hf == 0 else at((x + k) % 4, y, c)
        return pltpu.make_async_remote_copy(
            src_ref=src, dst_ref=dst, send_sem=line_s.at[e, hf, k], recv_sem=line_r.at[e, hf, k],
            device_id=(to, z), device_id_type=MESH)

    TAG, UP, DOWN, GRAD, HGRAD = 0, 1, 2, 3, 4

    def row_msg(e, hf, k2):
        if e == TAG:
            return row_copy(e, hf, k2, reqs, tagr.at[hf, me8[hf]])
        g = beyond(hf, k2)[0]
        if e in (UP, DOWN):
            src, dst = ((usend, urecv), (dsend, drecv))[e - UP]
            return row_copy(e, hf, k2, src.at[hf, g], dst.at[hf, pl.ds(me8[hf] * 4, 4)])
        src, dst = ((gsend, grecv), (hsend, hrecv))[e - GRAD]
        return row_copy(e, hf, k2, src.at[hf, g], dst.at[hf, me8[hf]])

    def line_msg(e, hf, k):
        p = along[hf]
        if e in (UP, DOWN):
            src, dst = ((upb, umid), (dnb, dmid))[e - UP]
            return line_copy(e, hf, k, src.at[hf], dst.at[hf, p])
        src, dst = ((gmid, gpart), (hmid, hpart))[e - GRAD]
        return line_copy(e, hf, k, src.at[hf, (p + k) % 4], dst.at[hf, p])

    def each_row(e, what):
        def go(j, carry):
            k2 = (j * 3) % 8
            for hf in (0, 1):
                what(row_msg(e, hf, k2), hf, k2)
            return carry
        lax.fori_loop(1, 8, go, 0)

    def each_line(e, what):
        for k in (1, 3, 2):
            for hf in (0, 1):
                what(line_msg(e, hf, k))

    def row_arrived(e):
        each_row(e, lambda copy, hf, k2: copy.wait_recv())

    def line_arrived(e):
        each_line(e, lambda copy: copy.wait_recv())

    def row_sent(e):
        each_row(e, lambda copy, hf, k2: copy.wait_send())

    def line_sent(e):
        each_line(e, lambda copy: copy.wait_send())

    each_row(TAG, lambda copy, hf, k2: copy.start())
    for hf in (0, 1):
        tagr[hf, me8[hf]] = reqs[...]

    cp_up.wait()
    cp_dn.wait()
    RH = R // 2
    for l in range(OWN):
        mine = slot_v[...] == d * OWN + l
        rank = jnp.sum(jnp.where(mine, rank_v[...], 0), axis=1, keepdims=True)
        for hf in (0, 1):
            rows = slice(hf * RH, (hf + 1) * RH)
            keep = lax.broadcasted_iota(I32, (RH, HEAD), 0) + hf * RH < rank
            upb[hf, l] = jnp.where(keep, upf[l, rows, :], 0.0).astype(BF)
    each_line(UP, lambda copy: copy.start())
    for l in range(OWN):
        mine = slot_v[...] == d * OWN + l
        rank = jnp.sum(jnp.where(mine, rank_v[...], 0), axis=1, keepdims=True)
        for hf in (0, 1):
            rows = slice(hf * RH, (hf + 1) * RH)
            keep = lax.broadcasted_iota(I32, (RH, FEAT), 0) + hf * RH < rank
            dnb[hf, l] = jnp.where(keep, dnf[l, rows, :], 0.0).astype(BF)
    for hf in (0, 1):
        umid[hf, along[hf]] = upb[hf]
        dmid[hf, along[hf]] = dnb[hf]
    row_arrived(TAG)
    for hf in (0, 1):
        tag_v[hf] = tagr[hf, :, 0, :]
    cp_tag = pltpu.make_async_copy(tag_v, tag_s, sm_sem.at[1])
    cp_tag.start()
    cp_tag.wait()

    def wanted(hf, g, p):
        return tag_s[hf, g, owner(hf, p, across[hf], c)]

    def hand_on(e, mid, send, recv):
        line_arrived(e)

        def go(copy, hf, k2):
            g = beyond(hf, k2)[0]
            for p in range(4):
                send[hf, g, p] = mid[hf, p, jnp.maximum(wanted(hf, g, p) - 1, 0)]
            copy.start()

        each_row(e, go)
        for hf in (0, 1):
            for p in range(4):
                recv[hf, me8[hf] * 4 + p] = mid[hf, p, jnp.maximum(wanted(hf, me8[hf], p) - 1, 0)]

    hand_on(UP, umid, usend, urecv)
    each_line(DOWN, lambda copy: copy.start())
    cp_bi.wait()
    cp_tok.wait()
    cp_w.wait()

    def of_block(recv, b):
        o = slot_s[ba_s[b]] // OWN
        ox, oy, oc = o // 8, (o // 2) % 4, o % 2
        return [recv[0, (ox * 2 + oc) * 4 + oy], recv[1, (oy * 2 + oc) * 4 + ox]]

    def of_blocks(recv, *bs):
        return jnp.concatenate([part for b in bs for part in of_block(recv, b)], axis=0)

    half = (slice(0, BLK // 2), slice(BLK // 2, BLK))

    def ar_copy(q, k, dirn, src, dst):
        return pltpu.make_async_remote_copy(
            src_ref=src, dst_ref=dst, send_sem=ar_s.at[q, dirn, k], recv_sem=ar_r.at[q, dirn, k],
            device_id=(d, (right, left)[dirn]), device_id_type=MESH)

    def ar_msg(q, k, dirn):
        sgn = (1, -1)[dirn]
        if k == 0:
            p = (z + 4) % NZ
            lo = (0, BLK // 2)[dirn]
            return ar_copy(q, k, dirn, arp.at[q, p, pl.ds(lo, BLK // 2)], arr.at[q, dirn, 0, pl.ds(lo, BLK // 2)])
        if k < 4:
            p = (z + sgn * (4 - k) + NZ) % NZ
            return ar_copy(q, k, dirn, arp.at[q, p], arr.at[q, dirn, k])
        p = (z - sgn * (k - 4) + NZ) % NZ
        if k < 7:
            return ar_copy(q, k, dirn, tot.at[q, p], tot.at[q, p])
        lo = (0, BLK // 2)[dirn]
        part = tot.at[q, p, pl.ds(lo, BLK // 2)]
        return ar_copy(q, k, dirn, part, part)

    def ar_step(q, k):
        if k > 0:
            for dirn in (0, 1):
                ar_msg(q, k - 1, dirn).wait_recv()
        if k in (1, 2, 3):
            for dirn in (0, 1):
                p = (z + (1, -1)[dirn] * (4 - k) + NZ) % NZ
                rows = half[dirn] if k == 1 else slice(0, BLK)
                arp[q, p, rows] = (arp[q, p, rows].astype(F32) + arr[q, dirn, k - 1, rows].astype(F32)).astype(BF)
        if k == 4:
            tot[q, z] = (arp[q, z].astype(F32) + arr[q, 0, 3].astype(F32) + arr[q, 1, 3].astype(F32)).astype(BF)
        if k < 8:
            for dirn in (0, 1):
                ar_msg(q, k, dirn).start()

    def ar_sent(q):
        for k in range(8):
            for dirn in (0, 1):
                ar_msg(q, k, dirn).wait_send()

    def scale_all(q):
        def go(j, carry):
            scaled[q, j] = (scale[pl.ds(j, 1), :] * tot[q, j].astype(F32)).astype(BF)
            return carry
        lax.fori_loop(0, NZ, go, 0)

    lanes = lax.broadcasted_iota(I32, (BLK, 2 * R), 1)

    def rows_of(b, n=BLK):
        return pl.ds(pl.multiple_of(b * n, n), n)

    def low_rank(q, recv, data, lo, hi):
        def go(j, carry):
            parts = [dot(data(2 * j + k), of_blocks(recv, 2 * j + k), 1, 1) for k in (0, 1)]
            arp[q, j] = jnp.concatenate(parts, axis=1).astype(BF)
            return carry

        lax.fori_loop(lo, hi, go, 0)

    def tok_of(b):
        return tok[rows_of(b), :]

    def cot_of(b):
        return cotf[z, rows_of(b), :]

    def send_grads(e, src, send, recv):
        def pick(hf, q, core, p):
            return src[hf, bi_s[0, owner(hf, p, q, core)]]

        def go(copy, hf, k2):
            g = beyond(hf, k2)[0]
            for p in range(4):
                send[hf, g, p] = pick(hf, g // 2, g % 2, p)
            copy.start()

        each_row(e, go)
        for hf in (0, 1):
            for p in range(4):
                recv[hf, me8[hf], p] = pick(hf, across[hf], c, p)

    def choose(hf):
        shape = (OWN * RH, 8 * RH)
        to, frm = lax.broadcasted_iota(I32, shape, 0), lax.broadcasted_iota(I32, shape, 1)
        same_row = (to % RH) == (frm % RH)
        slot, core = to // RH + 1, frm // RH

        def place(p, carry):
            tags = jnp.zeros(shape, I32)
            for g in range(8):
                tags = jnp.where(core == g, wanted(hf, g, p), tags)
            picks[hf, p] = jnp.where(same_row & (tags == slot), 1.0, 0.0).astype(BF)
            return carry

        lax.fori_loop(0, 4, place, 0)

    def tally(e, recv, mid, part, halves=(0, 1)):
        for hf in halves:
            def place(p, carry):
                pieces = jnp.concatenate([recv[hf, g, p] for g in range(8)], axis=0)
                sums = dot(picks[hf, p], pieces, 1, 0).astype(BF)
                for l in range(OWN):
                    mid[hf, p, l] = sums[l * RH:(l + 1) * RH]
                return carry
            lax.fori_loop(0, 4, place, 0)
            for k in (1, 3, 2):
                line_msg(e, hf, k).start()
            part[hf, along[hf]] = mid[hf, along[hf]]

    def total(e, part, acc):
        line_arrived(e)
        for hf in (0, 1):
            rows = slice(hf * RH, (hf + 1) * RH)
            for l in range(OWN):
                acc[l, rows, :] = sum(part[hf, p, l].astype(F32) for p in range(4))

    def down_grads():
        scale_all(0)

        def go(j, carry):
            turned = jnp.transpose(scaled[0, j].astype(F32)).astype(BF)
            for k in (0, 1):
                b = 2 * j + k
                piece = dot(turned[k * R:(k + 1) * R], tok_of(b), 1, 0).astype(BF)
                for hf in (0, 1):
                    grads[hf, b] = piece[hf * RH:(hf + 1) * RH]
            return carry

        lax.fori_loop(0, NZ, go, 0)

    def up_grads():
        scale_all(1)

        def go(j, carry):
            mine = scaled[1, j]
            turned = jnp.transpose(mine.astype(F32)).astype(BF)
            for k in (0, 1):
                b = 2 * j + k
                piece = dot(turned[k * R:(k + 1) * R], cot_of(b), 1, 0).astype(BF)
                for hf in (0, 1):
                    hgrads[hf, b] = piece[hf * RH:(hf + 1) * RH]
            return carry

        lax.fori_loop(0, NZ, go, 0)

    def apart(mine):
        zero = jnp.zeros((), BF)
        return jnp.concatenate([jnp.where(lanes < R, mine, zero), jnp.where(lanes >= R, mine, zero)], axis=0)

    def lora_values():
        def go(j, carry):
            ups = of_blocks(urecv, 2 * j, 2 * j + 1)
            lorav[rows_of(j, CH), :] = dot(apart(scaled[1, j]), ups, 1, 0).astype(BF)
            return carry

        lax.fori_loop(0, NZ, go, 0)

    def base_chunk(cc):
        rows = rows_of(cc, CH)
        part = dot(tok[rows, :], w[...], 1, 0)
        for k in range(NZ):
            base[k, rows, :] = part[:, k * HEAD:(k + 1) * HEAD].astype(BF)

    def tig_chunk(cc):
        rows = rows_of(cc, CH)
        full = jnp.concatenate([cotf[k, rows, :] for k in range(NZ)], axis=1)
        part = dot(full, w[...], 1, 1)
        lora = dot(apart(scaled[0, cc]), of_blocks(drecv, 2 * cc, 2 * cc + 1), 1, 0).astype(BF).astype(F32)
        tigv[rows, :] = (part + lora).astype(BF)

    def rs(n, h, cc, dirn):
        rows = rows_of(cc, CH)
        if dirn == 0:
            dest, to = (z + h) % NZ, right
        else:
            dest, to = (z - h + NZ) % NZ, left
        return pltpu.make_async_remote_copy(
            src_ref=base.at[dest, rows], dst_ref=rsr.at[dirn, n], send_sem=rs_s.at[dirn, n],
            recv_sem=rs_r.at[dirn, n], device_id=(d, to), device_id_type=MESH)

    def rs_add(n_in, h, cc, dirn):
        rs(n_in, h, cc, dirn).wait_recv()
        dest = (z + h) % NZ if dirn == 0 else (z - h + NZ) % NZ
        rows = rows_of(cc, CH)
        base[dest, rows, :] = (base[dest, rows, :].astype(F32) + rsr[dirn, n_in].astype(F32)).astype(BF)

    def ag_step(m):
        for dirn in (0, 1):
            lag = NC - (m // (3 * NC)) * (NC // 2) * dirn

            @pl.when(m >= NC)
            def _():
                ag(m - lag, dirn).wait_recv()
            ag(m - DEPTH, dirn).wait_send()
            ag(m, dirn).start()

    def rs_step(n):
        @pl.when(n < DEPTH)
        def _():
            for dirn in (0, 1):
                ag(MSG - DEPTH + n, dirn).wait_send()

        @pl.when(n >= DEPTH)
        def _():
            for dirn in (0, 1):
                rs(n - DEPTH, 3, 0, dirn).wait_send()

        @pl.when(n < 4)
        def _():
            for dirn in (0, 1):
                rs(n, 4, n + dirn * 4, dirn).start()

        @pl.when(n >= 4)
        def _():
            k, cc = (n - 4) // NC, (n - 4) % NC
            for dirn in (0, 1):
                @pl.when((k == 0) & (cc // 4 == dirn))
                def _():
                    rs_add(cc - 4 * dirn, 3, cc, dirn)

                @pl.when(k > 0)
                def _():
                    rs_add(n - NC, 3 - k, cc, dirn)
                rs(n, 3 - k, cc, dirn).start()

    def ag_rest(m, carry):
        ag(m, 0).wait_recv()
        ag(m - NC // 2 + (m // (3 * NC)) * (NC // 2), 1).wait_recv()
        return carry

    def every(u, first, step, n, what):
        @pl.when((u >= first) & (u < first + n * step) & ((u - first) % step == 0))
        def _():
            what((u - first) // step)

    def hops(u, first, q, lo, hi):
        for k in range(9):
            if lo <= first + k * HOPS[q] < hi:
                @pl.when(u == first + k * HOPS[q])
                def _():
                    ar_step(q, k)

    def run(lo, hi, step):
        def at_slot(first, what, *args):
            if lo <= first < hi:
                @pl.when(u_now[0] == first)
                def _():
                    what(*args)

        u_now = [None]

        def slot(u, carry):
            u_now[0] = u
            hops(u, U_BACK_HOP, 0, lo, hi)
            hops(u, U_LOW_HOP, 1, lo, hi)
            step(u)
            at_slot(U_BACK, row_arrived, UP)
            at_slot(U_BACK, low_rank, 0, urecv, cot_of, 0, NZ)
            at_slot(U_HAND, hand_on, DOWN, dmid, dsend, drecv)
            at_slot(U_LOW, row_arrived, DOWN)
            at_slot(U_LOW, low_rank, 1, drecv, tok_of, 0, NZ // 2)
            at_slot(U_LOW + 1, low_rank, 1, drecv, tok_of, NZ // 2, NZ)
            if lo < U_BASE + 2 * NC and U_BASE < hi:
                every(u, U_BASE, 2, NC, base_chunk)
            at_slot(U_BACK_END, down_grads)
            at_slot(U_BACK_END + 1, send_grads, GRAD, grads, gsend, grecv)
            at_slot(U_TIG, lax.fori_loop, MSG - NC, MSG, ag_rest, 0)
            if lo < U_TIG + 2 * NC and U_TIG < hi:
                every(u, U_TIG, 2, NC, tig_chunk)
            at_slot(U_TALLY, row_arrived, GRAD)
            at_slot(U_TALLY, tally, GRAD, grecv, gmid, gpart, (0,))
            at_slot(U_TALLY + 1, tally, GRAD, grecv, gmid, gpart, (1,))
            at_slot(U_LOW_END, up_grads)
            at_slot(U_LOW_END + 1, send_grads, HGRAD, hgrads, hsend, hrecv)
            at_slot(U_LOW_END + 2, lora_values)
            at_slot(U_SENT - 1, choose, 0)
            at_slot(U_SENT + 1, choose, 1)
            at_slot(U_SENT, row_sent, TAG)
            at_slot(U_SENT, line_sent, UP)
            at_slot(U_SENT + 2, row_sent, UP)
            at_slot(U_SENT + 4, line_sent, DOWN)
            at_slot(U_SENT + 8, row_sent, DOWN)
            at_slot(U_SENT + 10, ar_sent, 0)
            at_slot(U_TALLY + 4, row_sent, GRAD)
            at_slot(U_LOW_END + 3, ar_sent, 1)
            at_slot(U_HTALLY, row_arrived, HGRAD)
            at_slot(U_HTALLY, tally, HGRAD, hrecv, hmid, hpart)
            return carry

        lax.fori_loop(lo, hi, slot, 0)

    run(DEPTH, MSG, ag_step)
    run(MSG, 2 * MSG, lambda u: rs_step(u - MSG))

    def finish(cc, carry):
        n = MSG - NC + cc
        rows = rows_of(cc, CH)
        for dirn in (0, 1):
            rs(n, 1, cc, dirn).wait_recv()
        whole = base[z, rows, :].astype(F32) + rsr[0, n].astype(F32) + rsr[1, n].astype(F32)
        valv[rows, :] = (whole + lorav[rows, :].astype(F32)).astype(BF)
        return carry

    total(GRAD, gpart, dacc)
    lax.fori_loop(0, NC, finish, 0)
    total(HGRAD, hpart, uacc)

    def rs_rest(n, carry):
        for dirn in (0, 1):
            rs(n, 3, 0, dirn).wait_send()
        return carry

    lax.fori_loop(MSG - DEPTH, MSG, rs_rest, 0)
    for e in (GRAD, HGRAD):
        line_sent(e)
    row_sent(HGRAD)


def hand_out(*refs):
    n = len(refs) // 2
    copies = [pltpu.make_async_copy(refs[i], refs[n + i], refs[-1].at[i]) for i in range(n)]
    for copy in copies:
        copy.start()
    for copy in copies:
        copy.wait()


def on_device(tokens, cotangent, base_weight, adapter_down, adapter_up, block_adapter, adapter_slot, adapter_rank):
    vm, dma = pltpu.VMEM, pltpu.SemaphoreType.DMA
    smem = pl.BlockSpec(memory_space=pltpu.SMEM)
    vmem = pl.BlockSpec(memory_space=pltpu.VMEM)
    hbm = pl.BlockSpec(memory_space=pl.ANY)
    rh = R // 2
    scratch = [
        vm((ROWS, FEAT), BF), vm((NZ, ROWS, HEAD), BF), vm((FEAT, NZ * HEAD), BF),
        vm((OWN, R, FEAT), F32), vm((OWN, R, HEAD), F32), vm((2, OWN, rh, FEAT), BF), vm((2, OWN, rh, HEAD), BF),
        vm((NZ, ROWS, HEAD), BF), vm((2, MSG, CH, HEAD), BF),
        vm((8, 128), I32), vm((2, 8, 8, 128), I32), vm((2, 8, 128), I32), vm((8, 128), I32), vm((8, 128), F32),
        vm((2, 4, OWN, rh, HEAD), BF), vm((2, 8, 4, rh, HEAD), BF), vm((2, DP, rh, HEAD), BF),
        vm((2, 4, OWN, rh, FEAT), BF), vm((2, 8, 4, rh, FEAT), BF), vm((2, DP, rh, FEAT), BF),
        vm((2, NB, rh, FEAT), BF), vm((2, 8, 4, rh, FEAT), BF), vm((2, 8, 4, rh, FEAT), BF),
        vm((2, 4, OWN, rh, FEAT), BF), vm((2, 4, OWN, rh, FEAT), BF),
        vm((2, NB, rh, HEAD), BF), vm((2, 8, 4, rh, HEAD), BF), vm((2, 8, 4, rh, HEAD), BF),
        vm((2, 4, OWN, rh, HEAD), BF), vm((2, 4, OWN, rh, HEAD), BF),
        vm((2, NZ, BLK, 2 * R), BF), vm((2, 2, 4, BLK, 2 * R), BF), vm((2, NZ, BLK, 2 * R), BF), vm((2, NZ, BLK, 2 * R), BF),
        vm((ROWS, HEAD), BF), vm((2, 4, OWN * rh, 8 * rh), BF),
        pltpu.SMEM((2, 8, 128), I32), pltpu.SMEM((8, 128), I32),
        dma((5,)),
        dma((2, MSG)), dma((2, MSG)), dma((2, MSG)), dma((2, MSG)),
        dma((2, 2, 8)), dma((2, 2, 8)),
        dma((5, 2, 8)), dma((5, 2, 8)), dma((5, 2, 4)), dma((5, 2, 4)), dma((2,)),
    ]
    val, tig, dmg, umg = pl.pallas_call(
        kernel,
        out_shape=(
            vm((ROWS, HEAD), BF), vm((ROWS, FEAT), BF), vm((OWN, R, FEAT), F32), vm((OWN, R, HEAD), F32)),
        in_specs=[smem, smem, smem, vmem, vmem, hbm, hbm, hbm, hbm, hbm],
        out_specs=(vmem,) * 4,
        scratch_shapes=scratch,
        compiler_params=pltpu.CompilerParams(
            collective_id=0, has_side_effects=True, vmem_limit_bytes=54 * 2**20),
    )(
        block_adapter, adapter_slot, adapter_rank,
        adapter_slot.reshape(1, -1), adapter_rank.reshape(1, -1),
        tokens, cotangent, base_weight, jnp.swapaxes(adapter_down, 1, 2), adapter_up,
    )
    outs = (val, tig, dmg, umg)
    val, tig, dmg, umg = pl.pallas_call(
        hand_out,
        out_shape=tuple(jax.ShapeDtypeStruct(o.shape, o.dtype) for o in outs),
        in_specs=[vmem] * 4,
        out_specs=(hbm,) * 4,
        scratch_shapes=[dma((4,))],
        compiler_params=pltpu.CompilerParams(vmem_limit_bytes=4 * 2**20),
    )(*outs)
    return val, tig, jnp.swapaxes(dmg, 1, 2), umg


def solution(mesh):
    return jax.shard_map(
        on_device,
        mesh=mesh,
        in_specs=(
            P("dp", "tensor"), P("dp", "tensor"), P("tensor", None), P("dp", "tensor", None),
            P("dp", None, "tensor"), P("dp"), P(), P(),
        ),
        out_specs=(P("dp", "tensor"), P("dp", "tensor"), P("dp", "tensor", None), P("dp", None, "tensor")),
        check_vma=False,
    )
```
